128 devices in a mesh: wide: 16 (over z_hi, y, core), narrow: 8 (over z_lo, x).
Axes of the slice: x: 4, y: 4, z: 4 (z_hi: 2, z_lo: 2; z = z_hi * 2 + z_lo), core: 2. Of those that a mesh axis runs over, the one named last changes fastest.
Arguments:
- tokens: bfloat16 [6144, 5120], P('wide'), may hold values from -6 to 6
- norm_gain: float32 [5120], replicated, may hold values from 0.1 to 1.9
- w_query: bfloat16 [5120, 5120], P('wide', 'narrow'), may hold values from -0.078125 to 0.078125
- w_keyval: bfloat16 [5120, 2, 1024], P('wide', None, 'narrow'), may hold values from -0.078125 to 0.078125
- w_output: bfloat16 [5120, 5120], P('narrow', 'wide'), may hold values from -0.75 to 0.75
- prompt_cache: bfloat16 [16, 2, 8192, 1024], P(None, None, 'wide', 'narrow'), may hold values from -64 to 64
- stretch_lengths: int32 [16], replicated, may hold values from 1 to 1536, 6144 in all
- stretch_starts: int32 [16], replicated, may hold values from 0 to 2047
- page_route: int32 [16, 16], P('wide'), may hold values from 0 to 15, each once within a row
Outputs:
- attn_out: bfloat16 [6144, 5120], P('wide', 'narrow')
- decode_layout_cache: bfloat16 [8, 8, 2, 256, 32, 256], P('narrow', None, None, 'wide')
The draws below stay inside these ranges and needn't reach their ends.
Inputs may be any that keep to these rules, and one draw needn't show every extreme that they name: `stretch_lengths`: stretches sum to 6144 tokens; the longest has exactly 1536. `page_route`: each row is a permutation of 0 to 15.
All inputs are finite; a program needn't handle non-finite values.
Results may differ from the reference program's by a relative error of at most 0.017.
Values may be sent and summed in bfloat16 or wider, within the bound.
A program may use at most 128 MiB of HBM per device.

```python
import math
import jax
import jax.numpy as jnp
import numpy as np
from jax import lax

D = 5120
QH = 40
KVH = 8
HEAD_SIZE = 128
RELAID_LAYERS = 16
PAGE_POSITIONS = 32
NREQ = 16
TOKENS = 6144
P_SIZE = 8192
PB = 16
PAGE_SLOTS = 256
GROUP_KEY_HEADS = 2
MOST = 1536
N_WIDE = 16


def draw_prompt_cache(key, part):
    first = jax.random.fold_in(jax.random.fold_in(key, 7), 0)
    base = jax.random.normal(first, (RELAID_LAYERS, 2, P_SIZE, KVH * HEAD_SIZE), jnp.float32)
    return base.astype(jnp.bfloat16)


def plant(drawn, rng, smallest, top_value):
    spot = [jax.random.randint(jax.random.fold_in(rng, axis), (), 0, length) for axis, length in enumerate(drawn.shape)]
    longest = drawn.shape.index(max(drawn.shape))
    next_to = spot[:longest] + [(spot[longest] + 1) % drawn.shape[longest]] + spot[longest + 1:]
    return drawn.at[tuple(spot)].set(smallest).at[tuple(next_to)].set(top_value)


def block_scale(stream_key, extent, cuts, least, largest):
    level, own = 1.0, jax.random.fold_in(stream_key, 6)
    for position, shards_of in cuts:
        draws = jnp.exp(jax.random.uniform(jax.random.fold_in(own, position), (shards_of,), jnp.float32, least / len(cuts), largest / len(cuts)))
        level = level * jnp.repeat(draws, extent[position] // shards_of).reshape([-1 if axis == position else 1 for axis in range(len(extent))])
    return level


def split_up(count, total, bound, slope):
    loads = [(1 << 20) // math.isqrt(rank ** slope) + 1 for rank in range(2, count + 1)]
    spare, counts = total - bound - (count - 1), [1] * (count - 1)
    while spare > 0:
        candidates = [i for i in range(count - 1) if counts[i] < bound]
        pool, budget = sum([loads[i] for i in candidates]), spare
        for i in candidates:
            extra = min(bound - counts[i], max(1, budget * loads[i] // pool), spare)
            counts[i] = counts[i] + extra
            spare = spare - extra
    return np.array([bound] + counts)


def ragged_sizes(own_key, number_of, total, most, slope):
    if number_of == 2:
        one = jax.random.randint(own_key, (), max(1, total - most), min(most, total - 1) + 1)
        return jnp.stack([one, total - one])
    sizes = jnp.asarray(split_up(number_of, total, most, slope), jnp.int32)
    twos = (number_of - 1) // 2
    source_of, sink = sizes[1:1 + 2 * twos:2], sizes[2:2 + 2 * twos:2]
    margin = jnp.minimum(source_of - 1, most - sink)
    moved = jax.random.randint(jax.random.fold_in(own_key, 1), (twos,), 0, 1 << 20) % (margin + 1)
    sizes = sizes.at[1:1 + 2 * twos:2].set(source_of - moved).at[2:2 + 2 * twos:2].set(sink + moved)
    return sizes[jax.random.permutation(jax.random.fold_in(own_key, 2), number_of)]


def noise(own_key, shape, spread, most, cuts=(), kind=jnp.bfloat16):
    array = jax.random.normal(own_key, shape, jnp.float32) * spread
    if len(cuts) > 0:
        array = block_scale(own_key, shape, cuts, -0.22, 0.18) * array
    return jnp.clip(array, min=-most, max=most).astype(kind)


def setup_inputs(seed: int = 0) -> dict:
    seeds = jax.random.split(jax.random.key(seed), 10)
    tokens = noise(seeds[0], (TOKENS, D), 1.0, 6.0, ((0, 16),))
    norm_gain = jnp.clip(1.0 + 0.18 * jax.random.normal(seeds[1], (D,), jnp.float32), 0.1, 1.9)
    w_query = noise(seeds[2], (D, QH * HEAD_SIZE), D ** -0.5, 0.078125, ((0, 16), (1, 8)))
    w_keyval = noise(seeds[3], (D, 2, KVH * HEAD_SIZE), D ** -0.5, 0.078125, ((0, 16), (2, 8)))
    w_output = noise(seeds[4], (QH * HEAD_SIZE, D), 64 ** -0.5, 0.75, ((0, 8), (1, 16)))
    prompt_cache = draw_prompt_cache(jax.random.fold_in(seeds[9], 71), 0)
    stretch_lengths = ragged_sizes(seeds[6], NREQ, TOKENS, MOST, 2).astype(jnp.int32)
    stretch_starts = plant(jax.random.randint(seeds[7], (NREQ,), 0, 2048), jax.random.fold_in(seeds[7], 1), 0, 2047).astype(jnp.int32)
    page_route = jax.vmap(lambda own: jax.random.permutation(own, PB))(jax.random.split(seeds[8], N_WIDE)).reshape((N_WIDE, PB)).astype(jnp.int32)
    return dict(tokens=tokens, norm_gain=norm_gain, w_query=w_query, w_keyval=w_keyval, w_output=w_output, prompt_cache=prompt_cache, stretch_lengths=stretch_lengths, stretch_starts=stretch_starts, page_route=page_route)


def rotate(heads, positions):
    half = HEAD_SIZE // 2
    freq = 1000000.0 ** (-jnp.arange(half, dtype=jnp.float32) * 2.0 / HEAD_SIZE)
    angle = positions.astype(jnp.float32)[:, None] * freq[None, :]
    cosine = jnp.cos(angle)[:, None, :]
    sine = jnp.sin(angle)[:, None, :]
    first = heads[..., :half]
    second = heads[..., half:]
    return jnp.concatenate([first * cosine - second * sine, second * cosine + first * sine], -1)

def reference(tokens, norm_gain, w_query, w_keyval, w_output, prompt_cache, stretch_lengths, stretch_starts, page_route):
    xfull = tokens.astype(jnp.float32)
    normed = (xfull * lax.rsqrt(lax.optimization_barrier(jnp.mean(xfull * xfull, -1, keepdims=True)) + 1e-06) * norm_gain).astype(jnp.bfloat16)
    query = jnp.dot(normed, w_query, preferred_element_type=jnp.float32)
    keyval = jnp.dot(normed, w_keyval.reshape(D, 2 * KVH * HEAD_SIZE), preferred_element_type=jnp.float32).reshape(TOKENS, 2, KVH, HEAD_SIZE)
    ends = jnp.cumsum(stretch_lengths).astype(jnp.int32)
    begins = ends - stretch_lengths
    tok_index = jnp.arange(TOKENS, dtype=jnp.int32)
    seg = lax.optimization_barrier(jnp.sum((ends[None, :] <= tok_index[:, None]).astype(jnp.int32), 1)).astype(jnp.int32)
    pos = P_SIZE + stretch_starts[seg] + tok_index - begins[seg]
    rq = rotate(query.reshape(TOKENS, QH, HEAD_SIZE), pos).astype(jnp.bfloat16)
    rk = rotate(keyval[:, 0], pos).astype(jnp.bfloat16)
    rv = keyval[:, 1].astype(jnp.bfloat16)
    keys = jnp.concatenate([prompt_cache[0, 0].reshape(P_SIZE, KVH, HEAD_SIZE), rk], 0).astype(jnp.float32)
    vals = jnp.concatenate([prompt_cache[0, 1].reshape(P_SIZE, KVH, HEAD_SIZE), rv], 0).astype(jnp.float32)
    key_seg = jnp.concatenate([jnp.full((P_SIZE,), -1, jnp.int32), seg])
    key_tok = jnp.concatenate([jnp.zeros((P_SIZE,), jnp.int32), tok_index])
    group = QH // KVH
    qblock = math.gcd(TOKENS, 128)
    scale = HEAD_SIZE ** (-0.5)

    def one_block(index):
        first = index * qblock
        qpart = lax.dynamic_slice_in_dim(rq, first, qblock, 0).reshape(qblock, KVH, group, HEAD_SIZE).astype(jnp.float32)
        sseg = lax.dynamic_slice_in_dim(seg, first, qblock, 0)
        stok = lax.dynamic_slice_in_dim(tok_index, first, qblock, 0)
        score = jnp.einsum('tkgd,skd->kgts', qpart, keys) * scale
        visible = (key_seg[None, :] < 0) | (key_seg[None, :] == sseg[:, None]) & (key_tok[None, :] <= stok[:, None])
        masked = jnp.where(visible, score, -jnp.inf)
        top = lax.optimization_barrier(jnp.max(masked, -1, keepdims=True))
        ework = jnp.where(visible, jnp.exp(masked - top), 0.0)
        den = lax.optimization_barrier(jnp.sum(ework, -1))
        ebf = lax.optimization_barrier(ework.astype(jnp.bfloat16)).astype(jnp.float32)
        weighted = jnp.einsum('kgts,skd->kgtd', ebf, vals) / den[..., None]
        return jnp.transpose(weighted, (2, 0, 1, 3)).reshape(qblock, QH * HEAD_SIZE).astype(jnp.bfloat16)
    attn = lax.map(one_block, jnp.arange(TOKENS // qblock, dtype=jnp.int32)).reshape(TOKENS, QH * HEAD_SIZE)
    attn_out = jnp.dot(attn, w_output, preferred_element_type=jnp.float32).astype(jnp.bfloat16)
    pages = prompt_cache.reshape(RELAID_LAYERS, 2, N_WIDE, PB, PAGE_POSITIONS, KVH * HEAD_SIZE)
    inverse = jnp.argsort(page_route, axis=1).astype(jnp.int32)
    page_slots = jnp.arange(PAGE_SLOTS, dtype=jnp.int32)
    slot_block = page_slots % N_WIDE
    slot_rank = page_slots // N_WIDE
    chosen_pages = pages[:, :, slot_block, inverse[slot_block, slot_rank]]
    head_groups = KVH // GROUP_KEY_HEADS
    arranged_pages = chosen_pages.reshape(2, RELAID_LAYERS // 2, 2, PAGE_SLOTS, PAGE_POSITIONS, head_groups, GROUP_KEY_HEADS * HEAD_SIZE)
    decode_layout_cache = jnp.transpose(arranged_pages, (5, 0, 1, 2, 3, 4, 6)).reshape(2 * head_groups, RELAID_LAYERS // 2, 2, PAGE_SLOTS, PAGE_POSITIONS, GROUP_KEY_HEADS * HEAD_SIZE)
    return (attn_out, decode_layout_cache)
```

```python
import functools

import jax
import jax.numpy as jnp
from jax import lax
from jax.experimental import pallas as pl
from jax.experimental.pallas import tpu as pltpu
from jax.sharding import PartitionSpec as P

MESH = pl.DeviceIdType.MESH
HEAD = 128
GROUP = 5
REQUESTS = 16
WIDE = 16
NARROW = 8
BF16 = jnp.bfloat16
F32 = jnp.float32
KEYS = 1024
BACK = 4
LOG2E = 1.4426950408889634
MESSAGES = 17


def whole_kernel(
    tok_hbm,
    gain_ref,
    wqkv_hbm,
    wo_hbm,
    cache_hbm,
    freq_ref,
    lengths_ref,
    starts_ref,
    route_ref,
    out_ref,
    relay_ref,
    x_v,
    wqkv_v,
    kvp_v,
    wot_v,
    wo_v,
    comb_v,
    stage_v,
    proj_v,
    q_v,
    nkv_v,
    att_v,
    acc_v,
    top_v,
    den_v,
    cos_v,
    sin_v,
    begin_v,
    out_v,
    local_sem,
    g_send,
    g_recv,
    t_send,
    t_recv,
    x_send,
    x_recv,
    r_send,
    r_recv,
    n_send,
    n_recv,
    a_send,
    a_recv,
):
    tok_rows, depth = x_v.shape
    rows = wqkv_hbm.shape[0]
    cols = wqkv_hbm.shape[1]
    page_rows = comb_v.shape[3]
    half_layers = comb_v.shape[0]
    w = lax.axis_index("wide")
    n = lax.axis_index("narrow")
    core = lax.rem(w, 2)
    y = lax.rem(w // 2, 4)
    zh = w // 8
    plane = zh * 8

    def at_y(step):
        return plane + lax.rem(y + step, 4) * 2 + core

    def sib(chunk):
        return chunk + 1 - 2 * core

    def over_z(chunk):
        return lax.rem(chunk + 8, 16)

    yr, yl, y2 = at_y(1), at_y(3), at_y(2)
    par = lax.rem(n, 2)
    partner = n + 1 - 2 * par
    twin_w, twin_n = 2 * n + core, w // 2
    has_twin = twin_n != n

    half_at = pl.multiple_of(par * HEAD, HEAD)
    copies = [
        pltpu.make_async_copy(tok_hbm, x_v, local_sem.at[0]),
        pltpu.make_async_copy(
            wqkv_hbm, wqkv_v.at[pl.ds(pl.multiple_of(w * rows, 64), rows)], local_sem.at[1]
        ),
        pltpu.make_async_copy(
            cache_hbm.at[pl.ds(par * half_layers, half_layers)],
            comb_v.at[:, :, :, :, pl.ds(half_at, HEAD)],
            local_sem.at[2],
        ),
        pltpu.make_async_copy(cache_hbm.at[0], kvp_v.at[w], local_sem.at[3]),
    ]
    for copy in copies:
        copy.start()

    barrier = pltpu.get_barrier_semaphore()

    def greet_wide(k, carry):
        pl.semaphore_signal(barrier, inc=1, device_id=(lax.rem(w + k, WIDE), n), device_id_type=MESH)
        return carry

    def greet_narrow(k, carry):
        pl.semaphore_signal(barrier, inc=1, device_id=(w, lax.rem(n + k, NARROW)), device_id_type=MESH)
        return carry

    lax.fori_loop(1, WIDE, greet_wide, 0)
    lax.fori_loop(1, NARROW, greet_narrow, 0)

    peers = WIDE - 1 + NARROW - 1

    @pl.when(has_twin)
    def _():
        pl.semaphore_signal(barrier, inc=1, device_id=(twin_w, twin_n), device_id_type=MESH)
        pl.semaphore_wait(barrier, peers + 1)

    @pl.when(jnp.logical_not(has_twin))
    def _():
        pl.semaphore_wait(barrier, peers)

    def twin_copy():
        return pltpu.make_async_remote_copy(
            src_ref=wo_hbm, dst_ref=wot_v, send_sem=t_send, recv_sem=t_recv,
            device_id=(twin_w, twin_n), device_id_type=MESH,
        )

    own_wo = pltpu.make_async_copy(wo_hbm, wot_v, local_sem.at[4])

    @pl.when(has_twin)
    def _():
        twin_copy().start()

    @pl.when(jnp.logical_not(has_twin))
    def _():
        own_wo.start()

    def row_view(ref):
        def view(chunk, part=None):
            first = pl.multiple_of(chunk * rows, 64)
            if part is None:
                return ref.at[pl.ds(first, rows)]
            return ref.at[pl.ds(pl.multiple_of(first + part * (rows // 2), 32), rows // 2)]

        return view

    def prompt_view(chunk, part=None):
        return kvp_v.at[chunk] if part is None else kvp_v.at[chunk, part]

    views = [row_view(wqkv_v), prompt_view, row_view(wo_v)]
    owns = [wqkv_hbm, cache_hbm.at[0], wot_v]
    started = []

    def message(a, kind, chunk, part, to, own=False):
        dst = views[a](chunk, part)
        return pltpu.make_async_remote_copy(
            src_ref=owns[a] if own else dst,
            dst_ref=dst,
            send_sem=g_send.at[a, kind],
            recv_sem=g_recv.at[a, kind],
            device_id=(to, n),
            device_id_type=MESH,
        )

    def send(a, kind, chunk, part, to, own=False):
        copy = message(a, kind, chunk, part, to, own)
        copy.start()
        started.append(copy)

    def arrived(a, kind, chunk, part=None):
        message(a, kind, chunk, part, w).wait_recv()

    def first(a):
        send(a, 1, w, None, over_z(w), True)
        send(a, 2, w, None, yr, True)
        send(a, 3, w, None, yl, True)
        send(a, 0, w, None, sib(w), True)

    def second(a):
        chunk = over_z(w)
        arrived(a, 1, chunk)
        send(a, 5, chunk, None, yr)
        send(a, 6, chunk, None, yl)
        send(a, 4, chunk, None, sib(w))

    def third(a):
        arrived(a, 2, yl)
        send(a, 8, yl, 0, yr)
        send(a, 7, yl, None, sib(w))
        arrived(a, 3, yr)
        send(a, 10, yr, 1, yl)
        send(a, 9, yr, None, sib(w))

    def fourth(a):
        left, right = over_z(yl), over_z(yr)
        arrived(a, 5, left)
        send(a, 12, left, 0, yr)
        send(a, 11, left, None, sib(w))
        arrived(a, 6, right)
        send(a, 14, right, 1, yl)
        send(a, 13, right, None, sib(w))

    def fifth(a):
        arrived(a, 8, y2, 0)
        arrived(a, 10, y2, 1)
        send(a, 15, y2, None, sib(w))
        far = over_z(y2)
        arrived(a, 12, far, 0)
        arrived(a, 14, far, 1)
        send(a, 16, far, None, sib(w))

    def finish(a):
        for kind, chunk in (
            (0, w), (4, over_z(w)), (7, yl), (9, yr),
            (11, over_z(yl)), (13, over_z(yr)), (15, y2), (16, over_z(y2)),
        ):
            arrived(a, kind, sib(chunk))

    exchange = pltpu.make_async_remote_copy(
        src_ref=cache_hbm.at[pl.ds((1 - par) * half_layers, half_layers)],
        dst_ref=comb_v.at[:, :, :, :, pl.ds(half_at, HEAD)],
        send_sem=x_send, recv_sem=x_recv, device_id=(w, partner), device_id_type=MESH,
    )
    first(0)
    first(1)
    exchange.start()

    tok_id = w * tok_rows + lax.broadcasted_iota(jnp.int32, (tok_rows, HEAD), 0)
    begin = jnp.zeros((tok_rows, HEAD), jnp.int32)
    off = jnp.zeros((tok_rows, HEAD), jnp.int32)
    edge = jnp.int32(0)
    for k in range(REQUESTS):
        inside = tok_id >= edge
        begin = jnp.where(inside, edge, begin)
        off = jnp.where(inside, starts_ref[k] - edge, off)
        edge = edge + lengths_ref[k]
    begin_v[...] = begin
    block_keys = kvp_v.shape[2] * kvp_v.shape[3]
    prompt_len = WIDE * block_keys
    angle = (prompt_len + off + tok_id).astype(F32) * freq_ref[...]
    cos_v[...] = jnp.cos(angle)
    lane = lax.broadcasted_iota(jnp.int32, (tok_rows, HEAD), 1)
    sin_v[...] = jnp.where(lane < HEAD // 2, -1.0, 1.0) * jnp.sin(angle)

    copies[0].wait()
    block = 32

    def norm_block(i, carry):
        at = pl.ds(pl.multiple_of(i * block, block), block)
        xf = x_v[at, :].astype(F32)
        mean = jnp.sum(xf * xf, -1, keepdims=True) * (1.0 / depth)
        x_v[at, :] = (xf * lax.rsqrt(mean + 1e-06) * gain_ref[...]).astype(BF16)
        return carry

    lax.fori_loop(0, tok_rows // block, norm_block, 0)

    second(0)
    third(0)

    @pl.when(has_twin)
    def _():
        twin_copy().wait_recv()

    @pl.when(jnp.logical_not(has_twin))
    def _():
        own_wo.wait()

    first(2)
    own_wo2 = pltpu.make_async_copy(wot_v, views[2](w), local_sem.at[5])
    own_wo2.start()
    second(1)
    fourth(0)
    third(1)
    second(2)
    fifth(0)
    third(2)
    finish(0)
    copies[1].wait()

    proj_v[...] = jnp.zeros_like(proj_v)
    step = 1280

    def project(i, carry):
        at = pl.ds(pl.multiple_of(i * step, step), step)
        proj_v[...] += jnp.dot(x_v[:, at], wqkv_v[at, :], preferred_element_type=F32)
        return carry

    lax.fori_loop(0, depth // step, project, 0)

    def rotated(heads):
        return (heads * cos_v[...] + pltpu.roll(heads, HEAD // 2, 1) * sin_v[...]).astype(BF16)

    nkv_v[0, 0] = rotated(proj_v[:, GROUP * HEAD : (GROUP + 1) * HEAD])
    nkv_v[0, 1] = proj_v[:, (GROUP + 1) * HEAD : (GROUP + 2) * HEAD].astype(BF16)
    back_copies = []
    for j in range(1, BACK + 1):
        copy = pltpu.make_async_remote_copy(
            src_ref=nkv_v.at[0], dst_ref=nkv_v.at[j],
            send_sem=n_send.at[j], recv_sem=n_recv.at[j],
            device_id=(lax.rem(w + j, WIDE), n), device_id_type=MESH,
        )
        copy.start()
        back_copies.append(copy)
    for h in range(GROUP):
        q_v[h] = rotated(proj_v[:, h * HEAD : (h + 1) * HEAD])

    fourth(1)
    fifth(1)
    fourth(2)
    fifth(2)

    copies[2].wait()
    exchange.wait_recv()

    def relay_copy(k, to, source):
        return pltpu.make_async_remote_copy(
            src_ref=stage_v.at[to], dst_ref=relay_ref.at[0, :, :, source],
            send_sem=r_send.at[k], recv_sem=r_recv.at[k],
            device_id=(to, n), device_id_type=MESH,
        )

    def lay_out(k):
        to = lax.rem(w + k, WIDE)
        page = jnp.int32(0)
        for t in range(WIDE):
            page = jnp.where(route_ref[0, t] == to, jnp.int32(t), page)
        stage_v[to] = comb_v[:, :, page]
        return to

    def relay_step(k, carry):
        to = lay_out(k)
        relay_copy(k, to, w).start()
        return carry

    lax.fori_loop(1, WIDE, relay_step, 0)
    lay_out(0)
    own_page = pltpu.make_async_copy(stage_v.at[w], relay_ref.at[0, :, :, w], local_sem.at[6])
    own_page.start()

    finish(1)
    copies[3].wait()
    for copy in back_copies:
        copy.wait()

    factor = HEAD ** (-0.5) * LOG2E

    def attend(h, keys, vals, visible):
        score = lax.dot_general(
            q_v[h], keys, (((1,), (1,)), ((), ())), preferred_element_type=F32
        ) * factor
        if visible is not None:
            score = jnp.where(visible, score, -1e30)
        top = top_v[...]
        new_top = jnp.maximum(top, jnp.max(score, 1, keepdims=True))
        fall = jnp.exp2(top - new_top)
        weight = jnp.exp2(score - new_top[:, :1])
        part = weight[:, :HEAD]
        for i in range(1, weight.shape[1] // HEAD):
            part = part + weight[:, i * HEAD : (i + 1) * HEAD]
        den_v[...] = den_v[...] * fall + part
        acc_v[...] = acc_v[...] * fall + jnp.dot(
            weight.astype(BF16), vals, preferred_element_type=F32
        )
        top_v[...] = new_top

    per_step = KEYS // block_keys
    ring = (n // 4) * 4
    across = lax.rem(n + 4, NARROW)

    def around(k):
        return ring + lax.rem(n + k, 4)

    def head_copy(h, kind, owner, to):
        at = att_v.at[owner, :, pl.ds(pl.multiple_of(h * HEAD, HEAD), HEAD)]
        return pltpu.make_async_remote_copy(
            src_ref=at, dst_ref=at, send_sem=a_send.at[h, kind], recv_sem=a_recv.at[h, kind],
            device_id=(w, to), device_id_type=MESH,
        )

    def forward(h):
        head_copy(h, 3, across, n).wait_recv()
        head_copy(h, 4, across, around(1)).start()
        head_copy(h, 5, across, around(2)).start()
        head_copy(h, 6, across, around(3)).start()

    def head_step(h, carry):
        top_v[...] = jnp.full_like(top_v, -1e30)
        den_v[...] = jnp.zeros_like(den_v)
        acc_v[...] = jnp.zeros_like(acc_v)

        def prompt_step(i, inner):
            at = pl.ds(i * per_step, per_step)
            attend(h, kvp_v[at, 0].reshape(KEYS, HEAD), kvp_v[at, 1].reshape(KEYS, HEAD), None)
            return inner

        lax.fori_loop(0, WIDE // per_step, prompt_step, 0)

        def new_step(j, inner):
            key_id = (w - j) * tok_rows + lax.broadcasted_iota(jnp.int32, (tok_rows, tok_rows), 1)
            own_id = w * tok_rows + lax.broadcasted_iota(jnp.int32, (tok_rows, tok_rows), 0)
            visible = (key_id >= begin_v[:, :1]) & (key_id <= own_id)
            attend(h, nkv_v[j, 0], nkv_v[j, 1], visible)
            return inner

        lax.fori_loop(0, BACK + 1, new_step, 0)
        den = jnp.sum(den_v[...], 1, keepdims=True)
        att_v[n, :, pl.ds(pl.multiple_of(h * HEAD, HEAD), HEAD)] = (acc_v[...] / den).astype(BF16)
        head_copy(h, 3, n, across).start()
        head_copy(h, 0, n, around(1)).start()
        head_copy(h, 1, n, around(2)).start()
        head_copy(h, 2, n, around(3)).start()

        @pl.when(h > 0)
        def _():
            forward(h - 1)

        return carry

    lax.fori_loop(0, GROUP, head_step, 0)
    forward(GROUP - 1)

    finish(2)
    own_wo2.wait()
    out_v[...] = jnp.zeros_like(out_v)
    span = out_v.shape[1]

    def out_step(owner):
        at = pl.ds(pl.multiple_of(owner * span, span), span)
        out_v[...] += lax.dot_general(
            att_v[owner], wo_v[at, :], (((1,), (1,)), ((), ())), preferred_element_type=F32
        )

    def heads_in(kind, owner):
        def wait(h, carry):
            head_copy(h, kind, owner, n).wait_recv()
            return carry

        lax.fori_loop(0, GROUP, wait, 0)

    heads_in(0, around(3))
    heads_in(1, around(2))
    heads_in(2, around(1))

    def near_step(k, carry):
        out_step(around(k))
        return carry

    lax.fori_loop(0, 4, near_step, 0)
    far_ring = 4 - ring

    def beyond(k):
        return far_ring + lax.rem(n + k, 4)

    heads_in(4, beyond(3))
    heads_in(5, beyond(2))
    heads_in(6, beyond(1))

    def far_step(k, carry):
        out_step(beyond(k))
        return carry

    lax.fori_loop(0, 4, far_step, 0)
    out_ref[...] = out_v[...].astype(BF16)

    def sent(h, carry):
        head_copy(h, 3, n, across).wait_send()
        for kind in range(3):
            head_copy(h, kind, n, around(kind + 1)).wait_send()
            head_copy(h, kind + 4, across, around(kind + 1)).wait_send()
        return carry

    lax.fori_loop(0, GROUP, sent, 0)
    for copy in started:
        copy.wait_send()
    exchange.wait_send()

    @pl.when(has_twin)
    def _():
        twin_copy().wait_send()

    own_page.wait()

    def relay_end(k, carry):
        relay_copy(k, lax.rem(w + k, WIDE), w).wait_send()
        relay_copy(k, w, lax.rem(w - k + WIDE, WIDE)).wait_recv()
        return carry

    lax.fori_loop(1, WIDE, relay_end, 0)


def on_device(
    tokens,
    norm_gain,
    w_query,
    w_keyval,
    w_output,
    prompt_cache,
    stretch_lengths,
    stretch_starts,
    page_route,
):
    tok_rows, depth = tokens.shape
    rows, q_cols = w_query.shape
    layers, kinds, cache_rows, channels = prompt_cache.shape
    pages = page_route.shape[1]
    page_rows = cache_rows // pages
    half = layers // 2
    cols = q_cols + 2 * channels
    wqkv = jnp.concatenate([w_query, w_keyval.reshape(rows, 2 * channels)], 1)
    freq = 1000000.0 ** (-jnp.arange(HEAD // 2, dtype=jnp.float32) * 2.0 / HEAD)
    freq = jnp.concatenate([freq, freq])[None]
    any_spec = pl.BlockSpec(memory_space=pl.ANY)
    vmem_spec = pl.BlockSpec(memory_space=pltpu.VMEM)
    smem_spec = pl.BlockSpec(memory_space=pltpu.SMEM)
    cache5 = prompt_cache.reshape(layers, kinds, pages, page_rows, channels)
    dma = pltpu.SemaphoreType.DMA
    attn_out, relay = pl.pallas_call(
        whole_kernel,
        out_shape=(
            jax.ShapeDtypeStruct((tok_rows, q_cols), BF16),
            jax.ShapeDtypeStruct((1, half, kinds, WIDE, page_rows, 2 * channels), BF16),
        ),
        in_specs=[
            any_spec, vmem_spec, any_spec, any_spec, any_spec, vmem_spec,
            smem_spec, smem_spec, smem_spec,
        ],
        out_specs=(vmem_spec, any_spec),
        scratch_shapes=[
            pltpu.VMEM((tok_rows, depth), BF16),
            pltpu.VMEM((WIDE * rows, cols), BF16),
            pltpu.VMEM((WIDE, kinds, pages, page_rows, channels), BF16),
            pltpu.VMEM((rows, q_cols), BF16),
            pltpu.VMEM((WIDE * rows, q_cols), BF16),
            pltpu.VMEM((half, kinds, pages, page_rows, 2 * channels), BF16),
            pltpu.VMEM((WIDE, half, kinds, page_rows, 2 * channels), BF16),
            pltpu.VMEM((tok_rows, cols), F32),
            pltpu.VMEM((GROUP, tok_rows, HEAD), BF16),
            pltpu.VMEM((BACK + 1, 2, tok_rows, HEAD), BF16),
            pltpu.VMEM((NARROW, tok_rows, q_cols), BF16),
            pltpu.VMEM((tok_rows, HEAD), F32),
            pltpu.VMEM((tok_rows, HEAD), F32),
            pltpu.VMEM((tok_rows, HEAD), F32),
            pltpu.VMEM((tok_rows, HEAD), F32),
            pltpu.VMEM((tok_rows, HEAD), F32),
            pltpu.VMEM((tok_rows, HEAD), jnp.int32),
            pltpu.VMEM((tok_rows, q_cols), F32),
            dma((7,)),
            dma((3, MESSAGES)),
            dma((3, MESSAGES)),
            dma,
            dma,
            dma,
            dma,
            dma((WIDE,)),
            dma((WIDE,)),
            dma((BACK + 1,)),
            dma((BACK + 1,)),
            dma((GROUP, 7)),
            dma((GROUP, 7)),
        ],
        compiler_params=pltpu.CompilerParams(
            collective_id=0, has_side_effects=True, vmem_limit_bytes=60 * 2**20
        ),
    )(
        tokens, norm_gain[None], wqkv, w_output.T, cache5, freq,
        stretch_lengths, stretch_starts, page_route,
    )
    return attn_out, relay


def solution(mesh):
    placed = (
        P("wide", None),
        P(),
        P("wide", "narrow"),
        P("wide", None, "narrow"),
        P("narrow", "wide"),
        P(None, None, "wide", "narrow"),
        P(),
        P(),
        P("wide", None),
    )
    return jax.shard_map(
        on_device,
        mesh=mesh,
        in_specs=placed,
        out_specs=(P("wide", "narrow"), P("narrow", None, None, "wide", None, None)),
        check_vma=False,
    )
```

```python
import functools

import jax
import jax.numpy as jnp
from jax import lax
from jax.experimental import pallas as pl
from jax.experimental.pallas import tpu as pltpu
from jax.sharding import PartitionSpec as P

MESH = pl.DeviceIdType.MESH
HEAD = 128
GROUP = 5
REQUESTS = 16
WIDE = 16
NARROW = 8
BF16 = jnp.bfloat16
F32 = jnp.float32
KEYS = 1024
BACK = 4
LOG2E = 1.4426950408889634
MESSAGES = 17
PLANE = 8
PAIR = 2
PAIRS = PLANE // PAIR


def whole_kernel(
    tok_hbm,
    gain_ref,
    wqkv_hbm,
    wo_hbm,
    cache_hbm,
    freq_ref,
    lengths_ref,
    starts_ref,
    route_ref,
    out_ref,
    relay_ref,
    x_v,
    wqkv_v,
    kvp_v,
    wot_v,
    wo_v,
    cache_v,
    zsend_v,
    zrecv_v,
    xsend_v,
    ysend_v,
    proj_v,
    q_v,
    nkv_v,
    att_v,
    acc_v,
    top_v,
    den_v,
    cos_v,
    sin_v,
    begin_v,
    out_v,
    local_sem,
    g_send,
    g_recv,
    t_send,
    t_recv,
    x_send,
    x_recv,
    z_send,
    z_recv,
    f_sem,
    o_sem,
    r_send,
    r_recv,
    n_send,
    n_recv,
    a_send,
    a_recv,
):
    tok_rows, depth = x_v.shape
    rows = wqkv_hbm.shape[0]
    half_layers = xsend_v.shape[1]
    w = lax.axis_index("wide")
    n = lax.axis_index("narrow")
    core = lax.rem(w, 2)
    y = lax.rem(w // 2, 4)
    zh = w // 8
    plane = zh * 8

    def at_y(step):
        return plane + lax.rem(y + step, 4) * 2 + core

    def sib(chunk):
        return chunk + 1 - 2 * core

    def over_z(chunk):
        return lax.rem(chunk + 8, 16)

    yr, yl, y2 = at_y(1), at_y(3), at_y(2)
    par = lax.rem(n, 2)
    partner = n + 1 - 2 * par
    twin_w, twin_n = 2 * n + core, w // 2
    has_twin = twin_n != n

    half_at = pl.multiple_of(par * HEAD, HEAD)
    copies = [
        pltpu.make_async_copy(tok_hbm, x_v, local_sem.at[0]),
        pltpu.make_async_copy(
            wqkv_hbm, wqkv_v.at[pl.ds(pl.multiple_of(w * rows, 64), rows)], local_sem.at[1]
        ),
        pltpu.make_async_copy(cache_hbm, cache_v, local_sem.at[2]),
        pltpu.make_async_copy(cache_hbm.at[0], kvp_v.at[w], local_sem.at[3]),
    ]
    for copy in copies:
        copy.start()

    barrier = pltpu.get_barrier_semaphore()

    def greet_wide(k, carry):
        pl.semaphore_signal(barrier, inc=1, device_id=(lax.rem(w + k, WIDE), n), device_id_type=MESH)
        return carry

    def greet_narrow(k, carry):
        pl.semaphore_signal(barrier, inc=1, device_id=(w, lax.rem(n + k, NARROW)), device_id_type=MESH)
        return carry

    lax.fori_loop(1, WIDE, greet_wide, 0)
    lax.fori_loop(1, NARROW, greet_narrow, 0)

    peers = WIDE - 1 + NARROW - 1

    @pl.when(has_twin)
    def _():
        pl.semaphore_signal(barrier, inc=1, device_id=(twin_w, twin_n), device_id_type=MESH)
        pl.semaphore_wait(barrier, peers + 1)

    @pl.when(jnp.logical_not(has_twin))
    def _():
        pl.semaphore_wait(barrier, peers)

    def twin_copy():
        return pltpu.make_async_remote_copy(
            src_ref=wo_hbm, dst_ref=wot_v, send_sem=t_send, recv_sem=t_recv,
            device_id=(twin_w, twin_n), device_id_type=MESH,
        )

    own_wo = pltpu.make_async_copy(wo_hbm, wot_v, local_sem.at[4])

    @pl.when(has_twin)
    def _():
        twin_copy().start()

    @pl.when(jnp.logical_not(has_twin))
    def _():
        own_wo.start()

    def row_view(ref):
        def view(chunk, part=None):
            first = pl.multiple_of(chunk * rows, 64)
            if part is None:
                return ref.at[pl.ds(first, rows)]
            return ref.at[pl.ds(pl.multiple_of(first + part * (rows // 2), 32), rows // 2)]

        return view

    def prompt_view(chunk, part=None):
        return kvp_v.at[chunk] if part is None else kvp_v.at[chunk, part]

    views = [row_view(wqkv_v), prompt_view, row_view(wo_v)]
    owns = [wqkv_hbm, cache_hbm.at[0], wot_v]
    started = []

    def message(a, kind, chunk, part, to, own=False):
        dst = views[a](chunk, part)
        return pltpu.make_async_remote_copy(
            src_ref=owns[a] if own else dst,
            dst_ref=dst,
            send_sem=g_send.at[a, kind],
            recv_sem=g_recv.at[a, kind],
            device_id=(to, n),
            device_id_type=MESH,
        )

    def send(a, kind, chunk, part, to, own=False):
        copy = message(a, kind, chunk, part, to, own)
        copy.start()
        started.append(copy)

    def arrived(a, kind, chunk, part=None):
        message(a, kind, chunk, part, w).wait_recv()

    def first(a):
        send(a, 1, w, None, over_z(w), True)
        send(a, 2, w, None, yr, True)
        send(a, 3, w, None, yl, True)
        send(a, 0, w, None, sib(w), True)

    def second(a):
        chunk = over_z(w)
        arrived(a, 1, chunk)
        send(a, 5, chunk, None, yr)
        send(a, 6, chunk, None, yl)
        send(a, 4, chunk, None, sib(w))

    def third(a):
        arrived(a, 2, yl)
        send(a, 8, yl, 0, yr)
        send(a, 7, yl, None, sib(w))
        arrived(a, 3, yr)
        send(a, 10, yr, 1, yl)
        send(a, 9, yr, None, sib(w))

    def fourth(a):
        left, right = over_z(yl), over_z(yr)
        arrived(a, 5, left)
        send(a, 12, left, 0, yr)
        send(a, 11, left, None, sib(w))
        arrived(a, 6, right)
        send(a, 14, right, 1, yl)
        send(a, 13, right, None, sib(w))

    def fifth(a):
        arrived(a, 8, y2, 0)
        arrived(a, 10, y2, 1)
        send(a, 15, y2, None, sib(w))
        far = over_z(y2)
        arrived(a, 12, far, 0)
        arrived(a, 14, far, 1)
        send(a, 16, far, None, sib(w))

    def finish(a):
        for kind, chunk in (
            (0, w), (4, over_z(w)), (7, yl), (9, yr),
            (11, over_z(yl)), (13, over_z(yr)), (15, y2), (16, over_z(y2)),
        ):
            arrived(a, kind, sib(chunk))

    first(0)
    first(1)

    own_half = pl.ds(par * half_layers, half_layers)
    partner_half = pl.ds((1 - par) * half_layers, half_layers)
    own_lanes = pl.ds(half_at, HEAD)

    def z_copy(p):
        at = pl.ds(p * PAIR, PAIR)
        return pltpu.make_async_remote_copy(
            src_ref=zsend_v.at[at], dst_ref=zrecv_v.at[at],
            send_sem=z_send.at[p], recv_sem=z_recv.at[p],
            device_id=(over_z(w), n), device_id_type=MESH,
        )

    def near_x_copy():
        return pltpu.make_async_remote_copy(
            src_ref=xsend_v, dst_ref=ysend_v.at[0, :, :, :, :, own_lanes],
            send_sem=x_send.at[PAIRS], recv_sem=x_recv.at[PAIRS],
            device_id=(w, partner), device_id_type=MESH,
        )

    def far_x_copy(p):
        at = pl.ds(p * PAIR, PAIR)
        return pltpu.make_async_remote_copy(
            src_ref=zrecv_v.at[at, partner_half], dst_ref=ysend_v.at[1, at, :, :, :, own_lanes],
            send_sem=x_send.at[p], recv_sem=x_recv.at[p],
            device_id=(w, partner), device_id_type=MESH,
        )

    def far_own_copy(p):
        at = pl.ds(p * PAIR, PAIR)
        return pltpu.make_async_copy(
            zrecv_v.at[at, own_half], ysend_v.at[1, at, :, :, :, own_lanes], f_sem.at[p]
        )

    def page_for(to):
        page = jnp.int32(0)
        for t in range(WIDE):
            page = jnp.where(route_ref[0, t] == to, jnp.int32(t), page)
        return page

    copies[2].wait()

    def lay_far(d, carry):
        zsend_v[d] = cache_v[:, :, page_for(over_z(plane) + d)]
        return carry

    def lay_near(d, carry):
        page = page_for(plane + d)
        xsend_v[d] = cache_v[partner_half, :, page]
        ysend_v[0, d, :, :, :, own_lanes] = cache_v[own_half, :, page]
        return carry

    def z_step(p, carry):
        lax.fori_loop(p * PAIR, (p + 1) * PAIR, lay_far, 0)
        z_copy(p).start()
        return carry

    lax.fori_loop(0, PAIRS, z_step, 0)
    lax.fori_loop(0, PLANE, lay_near, 0)
    near_x_copy().start()

    def to_partner(p, carry):
        z_copy(p).wait_recv()
        far_x_copy(p).start()
        far_own_copy(p).start()
        return carry

    tok_id = w * tok_rows + lax.broadcasted_iota(jnp.int32, (tok_rows, HEAD), 0)
    begin = jnp.zeros((tok_rows, HEAD), jnp.int32)
    off = jnp.zeros((tok_rows, HEAD), jnp.int32)
    edge = jnp.int32(0)
    for k in range(REQUESTS):
        inside = tok_id >= edge
        begin = jnp.where(inside, edge, begin)
        off = jnp.where(inside, starts_ref[k] - edge, off)
        edge = edge + lengths_ref[k]
    begin_v[...] = begin
    block_keys = kvp_v.shape[2] * kvp_v.shape[3]
    prompt_len = WIDE * block_keys
    angle = (prompt_len + off + tok_id).astype(F32) * freq_ref[...]
    cos_v[...] = jnp.cos(angle)
    lane = lax.broadcasted_iota(jnp.int32, (tok_rows, HEAD), 1)
    sin_v[...] = jnp.where(lane < HEAD // 2, -1.0, 1.0) * jnp.sin(angle)

    copies[0].wait()
    block = 32

    def norm_block(i, carry):
        at = pl.ds(pl.multiple_of(i * block, block), block)
        xf = x_v[at, :].astype(F32)
        mean = jnp.sum(xf * xf, -1, keepdims=True) * (1.0 / depth)
        x_v[at, :] = (xf * lax.rsqrt(mean + 1e-06) * gain_ref[...]).astype(BF16)
        return carry

    lax.fori_loop(0, tok_rows // block, norm_block, 0)

    second(0)
    third(0)

    @pl.when(has_twin)
    def _():
        twin_copy().wait_recv()

    @pl.when(jnp.logical_not(has_twin))
    def _():
        own_wo.wait()

    first(2)
    own_wo2 = pltpu.make_async_copy(wot_v, views[2](w), local_sem.at[5])
    own_wo2.start()
    second(1)
    fourth(0)
    third(1)
    second(2)
    fifth(0)
    third(2)
    finish(0)
    copies[1].wait()

    proj_v[...] = jnp.zeros_like(proj_v)
    step = 1280

    def project(i, carry):
        at = pl.ds(pl.multiple_of(i * step, step), step)
        proj_v[...] += jnp.dot(x_v[:, at], wqkv_v[at, :], preferred_element_type=F32)
        return carry

    lax.fori_loop(0, depth // step, project, 0)

    def rotated(heads):
        return (heads * cos_v[...] + pltpu.roll(heads, HEAD // 2, 1) * sin_v[...]).astype(BF16)

    nkv_v[0, core, 0] = rotated(proj_v[:, GROUP * HEAD : (GROUP + 1) * HEAD])
    nkv_v[0, core, 1] = proj_v[:, (GROUP + 1) * HEAD : (GROUP + 2) * HEAD].astype(BF16)

    def back_copy(kind, slot, slot_to, which, to):
        return pltpu.make_async_remote_copy(
            src_ref=nkv_v.at[slot, which], dst_ref=nkv_v.at[slot_to, which],
            send_sem=n_send.at[kind], recv_sem=n_recv.at[kind],
            device_id=(to, n), device_id_type=MESH,
        )

    back_copies = [
        back_copy(1, 0, 1, core, lax.rem(w + 2, WIDE)),
        back_copy(2, 0, 2, core, lax.rem(w + 4, WIDE)),
        back_copy(0, 0, 0, core, sib(w)),
        back_copy(3, 1, 1, core, sib(w)),
        back_copy(4, 2, 2, core, sib(w)),
    ]
    for copy in back_copies[:3]:
        copy.start()
    for h in range(GROUP):
        q_v[h] = rotated(proj_v[:, h * HEAD : (h + 1) * HEAD])

    fourth(1)
    lax.fori_loop(0, PAIRS // 2, to_partner, 0)
    back_copies[0].wait_recv()
    back_copies[3].start()
    fifth(1)
    back_copies[1].wait_recv()
    back_copies[4].start()
    fourth(2)
    lax.fori_loop(PAIRS // 2, PAIRS, to_partner, 0)

    place = w - plane

    def source_of(s):
        return w if s == 0 else over_z(w)

    def y_copy(s, k, d, source):
        return pltpu.make_async_remote_copy(
            src_ref=ysend_v.at[s, d], dst_ref=relay_ref.at[0, :, :, source],
            send_sem=r_send.at[s, k], recv_sem=r_recv.at[s, k],
            device_id=(plane + d, n), device_id_type=MESH,
        )

    def to_owners(s):
        def step(k, carry):
            y_copy(s, k, lax.rem(place + k, PLANE), source_of(s)).start()
            return carry

        lax.fori_loop(1, PLANE, step, 0)

    def own_page(s):
        return pltpu.make_async_copy(
            ysend_v.at[s, place], relay_ref.at[0, :, :, source_of(s)], o_sem.at[s]
        )

    near_x_copy().wait_recv()
    to_owners(0)
    own_page(0).start()
    fifth(2)
    finish(1)
    copies[3].wait()
    for kind, slot, copy in ((0, 0, 2), (3, 1, 3), (4, 2, 4)):
        back_copy(kind, slot, slot, 1 - core, sib(w)).wait_recv()

    factor = HEAD ** (-0.5) * LOG2E

    def attend(h, keys, vals, visible):
        score = lax.dot_general(
            q_v[h], keys, (((1,), (1,)), ((), ())), preferred_element_type=F32
        ) * factor
        if visible is not None:
            score = jnp.where(visible, score, -1e30)
        top = top_v[...]
        new_top = jnp.maximum(top, jnp.max(score, 1, keepdims=True))
        fall = jnp.exp2(top - new_top)
        weight = jnp.exp2(score - new_top[:, :1])
        part = weight[:, :HEAD]
        for i in range(1, weight.shape[1] // HEAD):
            part = part + weight[:, i * HEAD : (i + 1) * HEAD]
        den_v[...] = den_v[...] * fall + part
        acc_v[...] = acc_v[...] * fall + jnp.dot(
            weight.astype(BF16), vals, preferred_element_type=F32
        )
        top_v[...] = new_top

    per_step = KEYS // block_keys
    ring = (n // 4) * 4
    across = lax.rem(n + 4, NARROW)

    def around(k):
        return ring + lax.rem(n + k, 4)

    far_ring = 4 - ring

    def beyond(k):
        return far_ring + lax.rem(n + k, 4)

    lead, trail = around(1), around(3)

    def head_copy(h, kind, owner, to):
        lanes = pl.ds(pl.multiple_of(h * HEAD, HEAD), HEAD)
        if kind < 5:
            at = att_v.at[owner, :, lanes]
        else:
            at = att_v.at[owner, pl.ds((kind + 1) % 2 * (tok_rows // 2), tok_rows // 2), lanes]
        return pltpu.make_async_remote_copy(
            src_ref=at, dst_ref=at, send_sem=a_send.at[h, kind], recv_sem=a_recv.at[h, kind],
            device_id=(w, to), device_id_type=MESH,
        )

    sends = (
        (0, n, lead, trail), (1, n, trail, lead), (2, n, across, across),
        (3, across, lead, beyond(3)), (4, across, trail, beyond(1)),
        (5, trail, lead, around(2)), (6, lead, trail, around(2)),
        (7, beyond(3), lead, beyond(2)), (8, beyond(1), trail, beyond(2)),
    )

    def give(h, *kinds):
        for kind in kinds:
            _, owner, to, _ = sends[kind]
            head_copy(h, kind, owner, to).start()

    def take(h, *kinds):
        for kind in kinds:
            head_copy(h, kind, sends[kind][3], n).wait_recv()

    def pass_on(h):
        take(h, 2)
        give(h, 3, 4)
        take(h, 0)
        give(h, 5)
        take(h, 1)
        give(h, 6)

    def pass_further(h):
        take(h, 3)
        give(h, 7)
        take(h, 4)
        give(h, 8)

    def head_step(h, carry):
        top_v[...] = jnp.full_like(top_v, -1e30)
        den_v[...] = jnp.zeros_like(den_v)
        acc_v[...] = jnp.zeros_like(acc_v)

        def prompt_step(i, inner):
            at = pl.ds(i * per_step, per_step)
            attend(h, kvp_v[at, 0].reshape(KEYS, HEAD), kvp_v[at, 1].reshape(KEYS, HEAD), None)
            return inner

        lax.fori_loop(0, WIDE // per_step, prompt_step, 0)

        def new_step(j, inner):
            key_id = (w - j) * tok_rows + lax.broadcasted_iota(jnp.int32, (tok_rows, tok_rows), 1)
            own_id = w * tok_rows + lax.broadcasted_iota(jnp.int32, (tok_rows, tok_rows), 0)
            visible = (key_id >= begin_v[:, :1]) & (key_id <= own_id)
            source = lax.rem(w - j + WIDE, WIDE)
            away = lax.rem(w // 2 - source // 2 + PLANE, PLANE)
            which = lax.rem(source, 2)
            attend(h, nkv_v[away, which, 0], nkv_v[away, which, 1], visible)
            return inner

        lax.fori_loop(0, BACK + 1, new_step, 0)
        den = jnp.sum(den_v[...], 1, keepdims=True)
        att_v[n, :, pl.ds(pl.multiple_of(h * HEAD, HEAD), HEAD)] = (acc_v[...] / den).astype(BF16)
        give(h, 2, 0, 1)

        @pl.when(h == 0)
        def _():
            def far_ready(p, inner):
                far_x_copy(p).wait_recv()
                far_own_copy(p).wait()
                return inner

            lax.fori_loop(0, PAIRS, far_ready, 0)
            to_owners(1)
            own_page(1).start()

        @pl.when(h > 0)
        def _():
            pass_on(h - 1)

        @pl.when(h > 1)
        def _():
            pass_further(h - 2)

        return carry

    lax.fori_loop(0, GROUP, head_step, 0)
    last = GROUP - 1
    pass_further(last - 1)
    pass_on(last)

    finish(2)
    own_wo2.wait()
    out_v[...] = jnp.zeros_like(out_v)
    span = out_v.shape[1]

    early = last * HEAD

    def earlier(h, carry):
        take(h, 5, 6, 7, 8)
        return carry

    lax.fori_loop(0, last, earlier, 0)

    def out_step(owner, carry, at=0, size=early):
        rows_at = pl.ds(pl.multiple_of(owner * span, span), span)
        out_v[...] += lax.dot_general(
            att_v[owner, :, at : at + size], wo_v[rows_at, at : at + size],
            (((1,), (1,)), ((), ())), preferred_element_type=F32,
        )
        return carry

    lax.fori_loop(0, NARROW // 2, out_step, 0)
    pass_further(last)
    lax.fori_loop(NARROW // 2, NARROW, out_step, 0)
    take(last, 5, 6, 7, 8)
    lax.fori_loop(0, NARROW, lambda owner, carry: out_step(owner, carry, early, HEAD), 0)
    out_ref[...] = out_v[...].astype(BF16)

    def sent(h, carry):
        for kind, owner, to, _ in sends:
            head_copy(h, kind, owner, to).wait_send()
        return carry

    lax.fori_loop(0, GROUP, sent, 0)
    for copy in started + back_copies:
        copy.wait_send()

    @pl.when(has_twin)
    def _():
        twin_copy().wait_send()

    def far_sent(p, carry):
        z_copy(p).wait_send()
        far_x_copy(p).wait_send()
        return carry

    lax.fori_loop(0, PAIRS, far_sent, 0)
    near_x_copy().wait_send()
    for s in range(2):
        own_page(s).wait()

        def relay_end(k, carry):
            y_copy(s, k, lax.rem(place + k, PLANE), source_of(s)).wait_send()
            giver = plane + lax.rem(place - k + PLANE, PLANE)
            y_copy(s, k, place, giver if s == 0 else over_z(giver)).wait_recv()
            return carry

        lax.fori_loop(1, PLANE, relay_end, 0)


def on_device(
    tokens,
    norm_gain,
    w_query,
    w_keyval,
    w_output,
    prompt_cache,
    stretch_lengths,
    stretch_starts,
    page_route,
):
    tok_rows, depth = tokens.shape
    rows, q_cols = w_query.shape
    layers, kinds, cache_rows, channels = prompt_cache.shape
    pages = page_route.shape[1]
    page_rows = cache_rows // pages
    half = layers // 2
    cols = q_cols + 2 * channels
    wqkv = jnp.concatenate([w_query, w_keyval.reshape(rows, 2 * channels)], 1)
    freq = 1000000.0 ** (-jnp.arange(HEAD // 2, dtype=jnp.float32) * 2.0 / HEAD)
    freq = jnp.concatenate([freq, freq])[None]
    any_spec = pl.BlockSpec(memory_space=pl.ANY)
    vmem_spec = pl.BlockSpec(memory_space=pltpu.VMEM)
    smem_spec = pl.BlockSpec(memory_space=pltpu.SMEM)
    cache5 = prompt_cache.reshape(layers, kinds, pages, page_rows, channels)
    dma = pltpu.SemaphoreType.DMA
    attn_out, relay = pl.pallas_call(
        whole_kernel,
        out_shape=(
            jax.ShapeDtypeStruct((tok_rows, q_cols), BF16),
            jax.ShapeDtypeStruct((1, half, kinds, WIDE, page_rows, 2 * channels), BF16),
        ),
        in_specs=[
            any_spec, vmem_spec, any_spec, any_spec, any_spec, vmem_spec,
            smem_spec, smem_spec, smem_spec,
        ],
        out_specs=(vmem_spec, any_spec),
        scratch_shapes=[
            pltpu.VMEM((tok_rows, depth), BF16),
            pltpu.VMEM((WIDE * rows, cols), BF16),
            pltpu.VMEM((WIDE, kinds, pages, page_rows, channels), BF16),
            pltpu.VMEM((rows, q_cols), BF16),
            pltpu.VMEM((WIDE * rows, q_cols), BF16),
            pltpu.VMEM((layers, kinds, pages, page_rows, channels), BF16),
            pltpu.VMEM((PLANE, layers, kinds, page_rows, channels), BF16),
            pltpu.VMEM((PLANE, layers, kinds, page_rows, channels), BF16),
            pltpu.VMEM((PLANE, half, kinds, page_rows, channels), BF16),
            pltpu.VMEM((2, PLANE, half, kinds, page_rows, 2 * channels), BF16),
            pltpu.VMEM((tok_rows, cols), F32),
            pltpu.VMEM((GROUP, tok_rows, HEAD), BF16),
            pltpu.VMEM((3, 2, 2, tok_rows, HEAD), BF16),
            pltpu.VMEM((NARROW, tok_rows, q_cols), BF16),
            pltpu.VMEM((tok_rows, HEAD), F32),
            pltpu.VMEM((tok_rows, HEAD), F32),
            pltpu.VMEM((tok_rows, HEAD), F32),
            pltpu.VMEM((tok_rows, HEAD), F32),
            pltpu.VMEM((tok_rows, HEAD), F32),
            pltpu.VMEM((tok_rows, HEAD), jnp.int32),
            pltpu.VMEM((tok_rows, q_cols), F32),
            dma((6,)),
            dma((3, MESSAGES)),
            dma((3, MESSAGES)),
            dma,
            dma,
            dma((PAIRS + 1,)),
            dma((PAIRS + 1,)),
            dma((PAIRS,)),
            dma((PAIRS,)),
            dma((PAIRS,)),
            dma((2,)),
            dma((2, PLANE)),
            dma((2, PLANE)),
            dma((5,)),
            dma((5,)),
            dma((GROUP, 9)),
            dma((GROUP, 9)),
        ],
        compiler_params=pltpu.CompilerParams(
            collective_id=0, has_side_effects=True, vmem_limit_bytes=60 * 2**20
        ),
    )(
        tokens, norm_gain[None], wqkv, w_output.T, cache5, freq,
        stretch_lengths, stretch_starts, page_route,
    )
    return attn_out, relay


def solution(mesh):
    placed = (
        P("wide", None),
        P(),
        P("wide", "narrow"),
        P("wide", None, "narrow"),
        P("narrow", "wide"),
        P(None, None, "wide", "narrow"),
        P(),
        P(),
        P("wide", None),
    )
    return jax.shard_map(
        on_device,
        mesh=mesh,
        in_specs=placed,
        out_specs=(P("wide", "narrow"), P("narrow", None, None, "wide", None, None)),
        check_vma=False,
    )
```

```python
import functools

import jax
import jax.numpy as jnp
from jax import lax
from jax.experimental import pallas as pl
from jax.experimental.pallas import tpu as pltpu
from jax.sharding import PartitionSpec as P

MESH = pl.DeviceIdType.MESH
HEAD = 128
GROUP = 5
REQUESTS = 16
WIDE = 16
NARROW = 8
BF16 = jnp.bfloat16
F32 = jnp.float32
KEYS = 2048
BACK = 4
LOG2E = 1.4426950408889634
MESSAGES = 17
PLANE = 8
PAIR = 2
PAIRS = PLANE // PAIR


def whole_kernel(
    tok_hbm,
    gain_ref,
    wqkv_hbm,
    wo_hbm,
    cache_hbm,
    freq_ref,
    lengths_ref,
    starts_ref,
    route_ref,
    out_ref,
    relay_ref,
    x_v,
    wqkv_v,
    kvp_v,
    wos_v,
    wot_v,
    wo_v,
    cache_v,
    zsend_v,
    zrecv_v,
    xsend_v,
    ysend_v,
    proj_v,
    q_v,
    nkv_v,
    att_v,
    acc_v,
    top_v,
    den_v,
    cos_v,
    sin_v,
    begin_v,
    out_v,
    local_sem,
    g_send,
    g_recv,
    t_send,
    t_recv,
    x_send,
    x_recv,
    z_send,
    z_recv,
    f_sem,
    o_sem,
    r_send,
    r_recv,
    n_send,
    n_recv,
    a_send,
    a_recv,
):
    tok_rows, depth = x_v.shape
    rows = wqkv_hbm.shape[0]
    half_layers = xsend_v.shape[1]
    w = lax.axis_index("wide")
    n = lax.axis_index("narrow")
    core = lax.rem(w, 2)
    y = lax.rem(w // 2, 4)
    zh = w // 8
    plane = zh * 8

    def at_y(step):
        return plane + lax.rem(y + step, 4) * 2 + core

    def sib(chunk):
        return chunk + 1 - 2 * core

    def over_z(chunk):
        return lax.rem(chunk + 8, 16)

    yr, yl, y2 = at_y(1), at_y(3), at_y(2)
    zw, zr, zl, z2 = over_z(w), over_z(yr), over_z(yl), over_z(y2)
    sw = sib(w)
    par = lax.rem(n, 2)
    partner = n + 1 - 2 * par
    x_at, z_at = lax.rem(n, 4), n // 4

    def mix(one, other):
        return one + other - 2 * one * other

    shift_w = mix(zh, z_at) * 8 + lax.rem(y + x_at, 4) * 2 + core
    shifts = n > 0
    turn_n = mix(zh, z_at) * 4 + lax.rem(y - x_at + 4, 4)
    turns = turn_n != n

    half_at = pl.multiple_of(par * HEAD, HEAD)
    copies = [
        pltpu.make_async_copy(tok_hbm, x_v, local_sem.at[0]),
        pltpu.make_async_copy(
            wqkv_hbm, wqkv_v.at[pl.ds(pl.multiple_of(w * rows, 64), rows)], local_sem.at[1]
        ),
        pltpu.make_async_copy(cache_hbm, cache_v, local_sem.at[2]),
        pltpu.make_async_copy(cache_hbm.at[0], kvp_v.at[w], local_sem.at[3]),
    ]
    for copy in copies:
        copy.start()

    barrier = pltpu.get_barrier_semaphore()

    def greet_wide(k, carry):
        pl.semaphore_signal(barrier, inc=1, device_id=(lax.rem(w + k, WIDE), n), device_id_type=MESH)
        return carry

    def greet_narrow(k, carry):
        pl.semaphore_signal(barrier, inc=1, device_id=(w, lax.rem(n + k, NARROW)), device_id_type=MESH)
        return carry

    lax.fori_loop(1, WIDE, greet_wide, 0)
    lax.fori_loop(1, NARROW, greet_narrow, 0)

    pl.semaphore_wait(barrier, WIDE - 1 + NARROW - 1)

    def shift_copy():
        return pltpu.make_async_remote_copy(
            src_ref=wo_hbm, dst_ref=wos_v, send_sem=t_send.at[0], recv_sem=t_recv.at[0],
            device_id=(shift_w, n), device_id_type=MESH,
        )

    def turn_copy():
        return pltpu.make_async_remote_copy(
            src_ref=wos_v, dst_ref=wot_v, send_sem=t_send.at[1], recv_sem=t_recv.at[1],
            device_id=(w, turn_n), device_id_type=MESH,
        )

    def shift_here():
        return pltpu.make_async_copy(wo_hbm, wos_v, local_sem.at[4])

    def turn_here():
        return pltpu.make_async_copy(wos_v, wot_v, local_sem.at[6])

    def either(moves, far, here):
        @pl.when(moves)
        def _():
            far()

        @pl.when(jnp.logical_not(moves))
        def _():
            here()

    either(shifts, lambda: shift_copy().start(), lambda: shift_here().start())

    def row_view(ref):
        def view(chunk, part=None):
            first = pl.multiple_of(chunk * rows, 64)
            if part is None:
                return ref.at[pl.ds(first, rows)]
            return ref.at[pl.ds(pl.multiple_of(first + part * (rows // 2), 32), rows // 2)]

        return view

    def prompt_view(chunk, part=None):
        return kvp_v.at[chunk] if part is None else kvp_v.at[chunk, part]

    views = [row_view(wqkv_v), prompt_view, row_view(wo_v)]
    owns = [wqkv_hbm, cache_hbm.at[0], wot_v]
    started = []

    def message(a, kind, chunk, part, to, own=False):
        dst = views[a](chunk, part)
        return pltpu.make_async_remote_copy(
            src_ref=owns[a] if own else dst,
            dst_ref=dst,
            send_sem=g_send.at[a, kind],
            recv_sem=g_recv.at[a, kind],
            device_id=(to, n),
            device_id_type=MESH,
        )

    def send(a, kind, chunk, part, to, own=False):
        message(a, kind, chunk, part, to, own).start()
        started.append((a, kind, chunk, part, to, own))

    def arrived(a, kind, chunk, part=None):
        message(a, kind, chunk, part, w).wait_recv()

    def first(a):
        send(a, 1, w, None, zw, True)
        send(a, 2, w, None, yr, True)
        send(a, 3, w, None, yl, True)
        send(a, 0, w, None, sw, True)

    def second(a):
        arrived(a, 1, zw)
        send(a, 5, zw, None, yr)
        send(a, 6, zw, None, yl)
        send(a, 4, zw, None, sw)

    def third(a):
        arrived(a, 2, yl)
        send(a, 8, yl, 0, yr)
        send(a, 7, yl, None, sw)
        arrived(a, 3, yr)
        send(a, 10, yr, 1, yl)
        send(a, 9, yr, None, sw)

    def fourth(a):
        arrived(a, 5, zl)
        send(a, 12, zl, 0, yr)
        send(a, 11, zl, None, sw)
        arrived(a, 6, zr)
        send(a, 14, zr, 1, yl)
        send(a, 13, zr, None, sw)

    def fifth(a):
        arrived(a, 8, y2, 0)
        arrived(a, 10, y2, 1)
        send(a, 15, y2, None, sw)
        arrived(a, 12, z2, 0)
        arrived(a, 14, z2, 1)
        send(a, 16, z2, None, sw)

    def finish(a):
        for kind, chunk in (
            (0, w), (4, over_z(w)), (7, yl), (9, yr),
            (11, over_z(yl)), (13, over_z(yr)), (15, y2), (16, over_z(y2)),
        ):
            arrived(a, kind, sib(chunk))

    first(0)
    first(1)

    own_half = pl.ds(par * half_layers, half_layers)
    partner_half = pl.ds((1 - par) * half_layers, half_layers)
    own_lanes = pl.ds(half_at, HEAD)

    def z_copy(p):
        at = pl.ds(p * PAIR, PAIR)
        return pltpu.make_async_remote_copy(
            src_ref=zsend_v.at[at], dst_ref=zrecv_v.at[at],
            send_sem=z_send.at[p], recv_sem=z_recv.at[p],
            device_id=(over_z(w), n), device_id_type=MESH,
        )

    def near_x_copy():
        return pltpu.make_async_remote_copy(
            src_ref=xsend_v, dst_ref=ysend_v.at[0, :, :, :, :, own_lanes],
            send_sem=x_send.at[PAIRS], recv_sem=x_recv.at[PAIRS],
            device_id=(w, partner), device_id_type=MESH,
        )

    def far_x_copy(p):
        at = pl.ds(p * PAIR, PAIR)
        return pltpu.make_async_remote_copy(
            src_ref=zrecv_v.at[at, partner_half], dst_ref=ysend_v.at[1, at, :, :, :, own_lanes],
            send_sem=x_send.at[p], recv_sem=x_recv.at[p],
            device_id=(w, partner), device_id_type=MESH,
        )

    def far_own_copy(p):
        at = pl.ds(p * PAIR, PAIR)
        return pltpu.make_async_copy(
            zrecv_v.at[at, own_half], ysend_v.at[1, at, :, :, :, own_lanes], f_sem.at[p]
        )

    def page_for(to):
        page = jnp.int32(0)
        for t in range(WIDE):
            page = jnp.where(route_ref[0, t] == to, jnp.int32(t), page)
        return page

    copies[2].wait()

    def lay_far(d, carry):
        zsend_v[d] = cache_v[:, :, page_for(over_z(plane) + d)]
        return carry

    def lay_near(d, carry):
        page = page_for(plane + d)
        xsend_v[d] = cache_v[partner_half, :, page]
        ysend_v[0, d, :, :, :, own_lanes] = cache_v[own_half, :, page]
        return carry

    lax.fori_loop(0, PLANE, lay_far, 0)
    lax.fori_loop(0, PLANE, lay_near, 0)

    def to_partner(p, carry):
        z_copy(p).wait_recv()
        far_x_copy(p).start()
        far_own_copy(p).start()
        return carry

    tok_id = w * tok_rows + lax.broadcasted_iota(jnp.int32, (tok_rows, HEAD), 0)
    begin = jnp.zeros((tok_rows, HEAD), jnp.int32)
    off = jnp.zeros((tok_rows, HEAD), jnp.int32)
    edge = jnp.int32(0)
    for k in range(REQUESTS):
        inside = tok_id >= edge
        begin = jnp.where(inside, edge, begin)
        off = jnp.where(inside, starts_ref[k] - edge, off)
        edge = edge + lengths_ref[k]
    begin_v[...] = begin
    block_keys = kvp_v.shape[2] * kvp_v.shape[3]
    prompt_len = WIDE * block_keys
    angle = (prompt_len + off + tok_id).astype(F32) * freq_ref[...]
    cos_v[...] = jnp.cos(angle)
    lane = lax.broadcasted_iota(jnp.int32, (tok_rows, HEAD), 1)
    sin_v[...] = jnp.where(lane < HEAD // 2, -1.0, 1.0) * jnp.sin(angle)

    copies[0].wait()
    block = 32

    def norm_block(i, carry):
        at = pl.ds(pl.multiple_of(i * block, block), block)
        xf = x_v[at, :].astype(F32)
        mean = jnp.sum(xf * xf, -1, keepdims=True) * (1.0 / depth)
        x_v[at, :] = (xf * lax.rsqrt(mean + 1e-06) * gain_ref[...]).astype(BF16)
        return carry

    lax.fori_loop(0, tok_rows // block, norm_block, 0)

    either(shifts, lambda: shift_copy().wait_recv(), lambda: shift_here().wait())
    either(turns, lambda: turn_copy().start(), lambda: turn_here().start())
    second(0)
    third(0)
    z_copy(0).start()
    second(1)
    fourth(0)
    third(1)
    z_copy(1).start()
    either(turns, lambda: turn_copy().wait_recv(), lambda: turn_here().wait())
    first(2)
    own_wo2 = pltpu.make_async_copy(wot_v, views[2](w), local_sem.at[5])
    own_wo2.start()
    near_x_copy().start()
    fifth(0)
    finish(0)
    copies[1].wait()
    fourth(1)
    second(2)
    z_copy(2).start()
    z_copy(3).start()

    proj_v[...] = jnp.zeros_like(proj_v)
    step = 1280

    def project(i, carry):
        at = pl.ds(pl.multiple_of(i * step, step), step)
        proj_v[...] += jnp.dot(x_v[:, at], wqkv_v[at, :], preferred_element_type=F32)
        return carry

    lax.fori_loop(0, depth // step, project, 0)

    def rotated(heads, times=1.0):
        turned = heads * cos_v[...] + pltpu.roll(heads, HEAD // 2, 1) * sin_v[...]
        return (turned * times).astype(BF16)

    nkv_v[0, core, 0] = rotated(proj_v[:, GROUP * HEAD : (GROUP + 1) * HEAD])
    nkv_v[0, core, 1] = proj_v[:, (GROUP + 1) * HEAD : (GROUP + 2) * HEAD].astype(BF16)

    def back_copy(kind, slot, slot_to, which, to):
        return pltpu.make_async_remote_copy(
            src_ref=nkv_v.at[slot, which], dst_ref=nkv_v.at[slot_to, which],
            send_sem=n_send.at[kind], recv_sem=n_recv.at[kind],
            device_id=(to, n), device_id_type=MESH,
        )

    back_copies = [
        back_copy(1, 0, 1, core, lax.rem(w + 2, WIDE)),
        back_copy(2, 0, 2, core, lax.rem(w + 4, WIDE)),
        back_copy(0, 0, 0, core, sib(w)),
        back_copy(3, 1, 1, core, sib(w)),
        back_copy(4, 2, 2, core, sib(w)),
    ]
    for copy in back_copies[:3]:
        copy.start()
    factor = HEAD ** (-0.5) * LOG2E
    for h in range(GROUP):
        q_v[h] = rotated(proj_v[:, h * HEAD : (h + 1) * HEAD], factor)

    third(2)
    back_copies[0].wait_recv()
    back_copies[3].start()
    fifth(1)
    back_copies[1].wait_recv()
    back_copies[4].start()
    lax.fori_loop(0, PAIRS // 2, to_partner, 0)

    place = w - plane

    def source_of(s):
        return w if s == 0 else over_z(w)

    def y_copy(s, k, d, source):
        return pltpu.make_async_remote_copy(
            src_ref=ysend_v.at[s, d], dst_ref=relay_ref.at[0, :, :, source],
            send_sem=r_send.at[s, k], recv_sem=r_recv.at[s, k],
            device_id=(plane + d, n), device_id_type=MESH,
        )

    def to_owners(s):
        def step(k, carry):
            y_copy(s, k, lax.rem(place + k, PLANE), source_of(s)).start()
            return carry

        lax.fori_loop(1, PLANE, step, 0)

    def own_page(s):
        return pltpu.make_async_copy(
            ysend_v.at[s, place], relay_ref.at[0, :, :, source_of(s)], o_sem.at[s]
        )

    near_x_copy().wait_recv()
    to_owners(0)
    own_page(0).start()
    finish(1)
    copies[3].wait()
    for kind, slot, copy in ((0, 0, 2), (3, 1, 3), (4, 2, 4)):
        back_copy(kind, slot, slot, 1 - core, sib(w)).wait_recv()

    def scores(h, keys):
        return lax.dot_general(q_v[h], keys, (((1,), (1,)), ((), ())), preferred_element_type=F32)

    def attend(score, vals):
        top = top_v[...]
        new_top = jnp.maximum(top, jnp.max(score, 1, keepdims=True))
        fall = jnp.exp2(top - new_top)
        weight = jnp.exp2(score - new_top[:, :1]).astype(BF16)
        both = jnp.concatenate([vals, jnp.ones(vals.shape, BF16)], 1)
        summed = jnp.dot(weight, both, preferred_element_type=F32)
        acc_v[...] = acc_v[...] * fall + summed[:, :HEAD]
        den_v[...] = den_v[...] * fall + summed[:, HEAD:]
        top_v[...] = new_top

    per_step = KEYS // block_keys
    ring = (n // 4) * 4
    across = lax.rem(n + 4, NARROW)

    def around(k):
        return ring + lax.rem(n + k, 4)

    far_ring = 4 - ring

    def beyond(k):
        return far_ring + lax.rem(n + k, 4)

    lead, trail = around(1), around(3)

    def head_copy(h, kind, owner, to):
        lanes = pl.ds(pl.multiple_of(h * HEAD, HEAD), HEAD)
        if kind < 5:
            at = att_v.at[owner, :, lanes]
        else:
            at = att_v.at[owner, pl.ds((kind + 1) % 2 * (tok_rows // 2), tok_rows // 2), lanes]
        return pltpu.make_async_remote_copy(
            src_ref=at, dst_ref=at, send_sem=a_send.at[h, kind], recv_sem=a_recv.at[h, kind],
            device_id=(w, to), device_id_type=MESH,
        )

    sends = (
        (0, n, lead, trail), (1, n, trail, lead), (2, n, across, across),
        (3, across, lead, beyond(3)), (4, across, trail, beyond(1)),
        (5, trail, lead, around(2)), (6, lead, trail, around(2)),
        (7, beyond(3), lead, beyond(2)), (8, beyond(1), trail, beyond(2)),
    )

    def give(h, *kinds):
        for kind in kinds:
            _, owner, to, _ = sends[kind]
            head_copy(h, kind, owner, to).start()

    def take(h, *kinds):
        for kind in kinds:
            head_copy(h, kind, sends[kind][3], n).wait_recv()

    def pass_on(h):
        take(h, 2)
        give(h, 3, 4)
        take(h, 0)
        give(h, 5)
        take(h, 1)
        give(h, 6)

    def pass_further(h):
        take(h, 3)
        give(h, 7)
        take(h, 4)
        give(h, 8)

    def head_step(h, carry):
        top_v[...] = jnp.full_like(top_v, -1e30)
        den_v[...] = jnp.zeros_like(den_v)
        acc_v[...] = jnp.zeros_like(acc_v)

        def prompt_step(i, inner):
            at = pl.ds(i * per_step, per_step)
            attend(scores(h, kvp_v[at, 0].reshape(KEYS, HEAD)), kvp_v[at, 1].reshape(KEYS, HEAD))
            return inner

        lax.fori_loop(0, WIDE // per_step, prompt_step, 0)

        slots = []
        for j in range(BACK + 1):
            source = lax.rem(w - j + WIDE, WIDE)
            slots.append((lax.rem(w // 2 - source // 2 + PLANE, PLANE), lax.rem(source, 2)))
        new_keys = jnp.concatenate([nkv_v[away, which, 0] for away, which in slots], 0)
        new_vals = jnp.concatenate([nkv_v[away, which, 1] for away, which in slots], 0)
        score = scores(h, new_keys)
        own_id = w * tok_rows + lax.broadcasted_iota(jnp.int32, (tok_rows, tok_rows), 0)
        masked = []
        for j in range(BACK + 1):
            key_id = (w - j) * tok_rows + lax.broadcasted_iota(jnp.int32, (tok_rows, tok_rows), 1)
            visible = key_id >= begin_v[:, :1]
            if j == 0:
                visible = visible & (key_id <= own_id)
            masked.append(jnp.where(visible, score[:, j * tok_rows : (j + 1) * tok_rows], -1e30))
        attend(jnp.concatenate(masked, 1), new_vals)
        att_v[n, :, pl.ds(pl.multiple_of(h * HEAD, HEAD), HEAD)] = (acc_v[...] / den_v[...]).astype(BF16)
        give(h, 2, 0, 1)

        @pl.when(h == 0)
        def _():
            fourth(2)
            lax.fori_loop(PAIRS // 2, PAIRS, to_partner, 0)

        @pl.when(h == 1)
        def _():
            fifth(2)

            def far_ready(p, inner):
                far_x_copy(p).wait_recv()
                far_own_copy(p).wait()
                return inner

            lax.fori_loop(0, PAIRS, far_ready, 0)
            to_owners(1)
            own_page(1).start()

        @pl.when(h > 0)
        def _():
            pass_on(h - 1)

        @pl.when(h > 1)
        def _():
            pass_further(h - 2)

        return carry

    lax.fori_loop(0, GROUP, head_step, 0)
    last = GROUP - 1
    pass_further(last - 1)
    pass_on(last)

    finish(2)
    own_wo2.wait()
    out_v[...] = jnp.zeros_like(out_v)
    span = out_v.shape[1]

    early = last * HEAD

    def earlier(h, carry):
        take(h, 5, 6, 7, 8)
        return carry

    lax.fori_loop(0, last, earlier, 0)

    def out_step(owner, carry, at=0, size=early):
        held = mix(owner // 4, z_at) * 4 + lax.rem(owner + x_at, 4)
        rows_at = pl.ds(pl.multiple_of(held * span, span), span)
        out_v[...] += lax.dot_general(
            att_v[owner, :, at : at + size], wo_v[rows_at, at : at + size],
            (((1,), (1,)), ((), ())), preferred_element_type=F32,
        )
        return carry

    lax.fori_loop(0, NARROW // 2, out_step, 0)
    pass_further(last)
    lax.fori_loop(NARROW // 2, NARROW, out_step, 0)
    take(last, 5, 6, 7, 8)
    lax.fori_loop(0, NARROW, lambda owner, carry: out_step(owner, carry, early, HEAD), 0)
    out_ref[...] = out_v[...].astype(BF16)

    def sent(h, carry):
        for kind, owner, to, _ in sends:
            head_copy(h, kind, owner, to).wait_send()
        return carry

    lax.fori_loop(0, GROUP, sent, 0)
    for sending in started:
        message(*sending).wait_send()
    for copy in back_copies:
        copy.wait_send()

    either(shifts, lambda: shift_copy().wait_send(), lambda: None)
    either(turns, lambda: turn_copy().wait_send(), lambda: None)

    def far_sent(p, carry):
        z_copy(p).wait_send()
        far_x_copy(p).wait_send()
        return carry

    lax.fori_loop(0, PAIRS, far_sent, 0)
    near_x_copy().wait_send()
    for s in range(2):
        own_page(s).wait()

        def relay_end(k, carry):
            y_copy(s, k, lax.rem(place + k, PLANE), source_of(s)).wait_send()
            giver = plane + lax.rem(place - k + PLANE, PLANE)
            y_copy(s, k, place, giver if s == 0 else over_z(giver)).wait_recv()
            return carry

        lax.fori_loop(1, PLANE, relay_end, 0)


def on_device(
    tokens,
    norm_gain,
    w_query,
    w_keyval,
    w_output,
    prompt_cache,
    stretch_lengths,
    stretch_starts,
    page_route,
):
    tok_rows, depth = tokens.shape
    rows, q_cols = w_query.shape
    layers, kinds, cache_rows, channels = prompt_cache.shape
    pages = page_route.shape[1]
    page_rows = cache_rows // pages
    half = layers // 2
    cols = q_cols + 2 * channels
    wqkv = jnp.concatenate([w_query, w_keyval.reshape(rows, 2 * channels)], 1)
    freq = 1000000.0 ** (-jnp.arange(HEAD // 2, dtype=jnp.float32) * 2.0 / HEAD)
    freq = jnp.concatenate([freq, freq])[None]
    any_spec = pl.BlockSpec(memory_space=pl.ANY)
    vmem_spec = pl.BlockSpec(memory_space=pltpu.VMEM)
    smem_spec = pl.BlockSpec(memory_space=pltpu.SMEM)
    cache5 = prompt_cache.reshape(layers, kinds, pages, page_rows, channels)
    dma = pltpu.SemaphoreType.DMA
    attn_out, relay = pl.pallas_call(
        whole_kernel,
        out_shape=(
            jax.ShapeDtypeStruct((tok_rows, q_cols), BF16),
            jax.ShapeDtypeStruct((1, half, kinds, WIDE, page_rows, 2 * channels), BF16),
        ),
        in_specs=[
            any_spec, vmem_spec, any_spec, any_spec, any_spec, vmem_spec,
            smem_spec, smem_spec, smem_spec,
        ],
        out_specs=(vmem_spec, any_spec),
        scratch_shapes=[
            pltpu.VMEM((tok_rows, depth), BF16),
            pltpu.VMEM((WIDE * rows, cols), BF16),
            pltpu.VMEM((WIDE, kinds, pages, page_rows, channels), BF16),
            pltpu.VMEM((rows, q_cols), BF16),
            pltpu.VMEM((rows, q_cols), BF16),
            pltpu.VMEM((WIDE * rows, q_cols), BF16),
            pltpu.VMEM((layers, kinds, pages, page_rows, channels), BF16),
            pltpu.VMEM((PLANE, layers, kinds, page_rows, channels), BF16),
            pltpu.VMEM((PLANE, layers, kinds, page_rows, channels), BF16),
            pltpu.VMEM((PLANE, half, kinds, page_rows, channels), BF16),
            pltpu.VMEM((2, PLANE, half, kinds, page_rows, 2 * channels), BF16),
            pltpu.VMEM((tok_rows, cols), F32),
            pltpu.VMEM((GROUP, tok_rows, HEAD), BF16),
            pltpu.VMEM((3, 2, 2, tok_rows, HEAD), BF16),
            pltpu.VMEM((NARROW, tok_rows, q_cols), BF16),
            pltpu.VMEM((tok_rows, HEAD), F32),
            pltpu.VMEM((tok_rows, HEAD), F32),
            pltpu.VMEM((tok_rows, HEAD), F32),
            pltpu.VMEM((tok_rows, HEAD), F32),
            pltpu.VMEM((tok_rows, HEAD), F32),
            pltpu.VMEM((tok_rows, HEAD), jnp.int32),
            pltpu.VMEM((tok_rows, q_cols), F32),
            dma((7,)),
            dma((3, MESSAGES)),
            dma((3, MESSAGES)),
            dma((2,)),
            dma((2,)),
            dma((PAIRS + 1,)),
            dma((PAIRS + 1,)),
            dma((PAIRS,)),
            dma((PAIRS,)),
            dma((PAIRS,)),
            dma((2,)),
            dma((2, PLANE)),
            dma((2, PLANE)),
            dma((5,)),
            dma((5,)),
            dma((GROUP, 9)),
            dma((GROUP, 9)),
        ],
        compiler_params=pltpu.CompilerParams(
            collective_id=0, has_side_effects=True, vmem_limit_bytes=60 * 2**20
        ),
    )(
        tokens, norm_gain[None], wqkv, w_output.T, cache5, freq,
        stretch_lengths, stretch_starts, page_route,
    )
    return attn_out, relay


def solution(mesh):
    placed = (
        P("wide", None),
        P(),
        P("wide", "narrow"),
        P("wide", None, "narrow"),
        P("narrow", "wide"),
        P(None, None, "wide", "narrow"),
        P(),
        P(),
        P("wide", None),
    )
    return jax.shard_map(
        on_device,
        mesh=mesh,
        in_specs=placed,
        out_specs=(P("wide", "narrow"), P("narrow", None, None, "wide", None, None)),
        check_vma=False,
    )
```

```python
import functools

import jax
import jax.numpy as jnp
from jax import lax
from jax.experimental import pallas as pl
from jax.experimental.pallas import tpu as pltpu
from jax.sharding import PartitionSpec as P

MESH = pl.DeviceIdType.MESH
HEAD = 128
GROUP = 5
REQUESTS = 16
WIDE = 16
NARROW = 8
BF16 = jnp.bfloat16
F32 = jnp.float32
KEYS = 2048
BACK = 4
LOG2E = 1.4426950408889634
MESSAGES = 17
PLANE = 8
PAIR = 2
PAIRS = PLANE // PAIR


def whole_kernel(
    tok_hbm,
    gain_ref,
    wqkv_hbm,
    wo_hbm,
    cache_hbm,
    freq_ref,
    lengths_ref,
    starts_ref,
    route_ref,
    out_ref,
    relay_ref,
    x_v,
    wqkv_v,
    kvp_v,
    wos_v,
    wot_v,
    wo_v,
    cache_v,
    zsend_v,
    zrecv_v,
    xsend_v,
    ysend_v,
    proj_v,
    q_v,
    nkv_v,
    att_v,
    acc_v,
    top_v,
    den_v,
    cos_v,
    sin_v,
    begin_v,
    out_v,
    local_sem,
    g_send,
    g_recv,
    t_send,
    t_recv,
    x_send,
    x_recv,
    z_send,
    z_recv,
    f_sem,
    o_sem,
    r_send,
    r_recv,
    n_send,
    n_recv,
    a_send,
    a_recv,
):
    tok_rows, depth = x_v.shape
    rows = wqkv_hbm.shape[0]
    half_layers = xsend_v.shape[1]
    w = lax.axis_index("wide")
    n = lax.axis_index("narrow")
    core = lax.rem(w, 2)
    y = lax.rem(w // 2, 4)
    zh = w // 8
    plane = zh * 8

    def at_y(step):
        return plane + lax.rem(y + step, 4) * 2 + core

    def sib(chunk):
        return chunk + 1 - 2 * core

    def over_z(chunk):
        return lax.rem(chunk + 8, 16)

    yr, yl, y2 = at_y(1), at_y(3), at_y(2)
    zw, zr, zl, z2 = over_z(w), over_z(yr), over_z(yl), over_z(y2)
    sw = sib(w)
    par = lax.rem(n, 2)
    partner = n + 1 - 2 * par
    x_at, z_at = lax.rem(n, 4), n // 4

    def mix(one, other):
        return one + other - 2 * one * other

    shift_w = mix(zh, z_at) * 8 + lax.rem(y + x_at, 4) * 2 + core
    shifts = n > 0
    turn_n = mix(zh, z_at) * 4 + lax.rem(y - x_at + 4, 4)
    turns = turn_n != n

    half_at = pl.multiple_of(par * HEAD, HEAD)
    copies = [
        pltpu.make_async_copy(tok_hbm, x_v, local_sem.at[0]),
        pltpu.make_async_copy(
            wqkv_hbm, wqkv_v.at[pl.ds(pl.multiple_of(w * rows, 64), rows)], local_sem.at[1]
        ),
        pltpu.make_async_copy(cache_hbm, cache_v, local_sem.at[2]),
        pltpu.make_async_copy(cache_hbm.at[0], kvp_v.at[w], local_sem.at[3]),
    ]
    for copy in copies:
        copy.start()

    barrier = pltpu.get_barrier_semaphore()

    def greet_wide(k, carry):
        pl.semaphore_signal(barrier, inc=1, device_id=(lax.rem(w + k, WIDE), n), device_id_type=MESH)
        return carry

    def greet_narrow(k, carry):
        pl.semaphore_signal(barrier, inc=1, device_id=(w, lax.rem(n + k, NARROW)), device_id_type=MESH)
        return carry

    lax.fori_loop(1, WIDE, greet_wide, 0)
    lax.fori_loop(1, NARROW, greet_narrow, 0)

    pl.semaphore_wait(barrier, WIDE - 1 + NARROW - 1)

    def shift_copy():
        return pltpu.make_async_remote_copy(
            src_ref=wo_hbm, dst_ref=wos_v, send_sem=t_send.at[0], recv_sem=t_recv.at[0],
            device_id=(shift_w, n), device_id_type=MESH,
        )

    def turn_copy():
        return pltpu.make_async_remote_copy(
            src_ref=wos_v, dst_ref=wot_v, send_sem=t_send.at[1], recv_sem=t_recv.at[1],
            device_id=(w, turn_n), device_id_type=MESH,
        )

    def shift_here():
        return pltpu.make_async_copy(wo_hbm, wos_v, local_sem.at[4])

    def turn_here():
        return pltpu.make_async_copy(wos_v, wot_v, local_sem.at[6])

    def either(moves, far, here):
        @pl.when(moves)
        def _():
            far()

        @pl.when(jnp.logical_not(moves))
        def _():
            here()

    either(shifts, lambda: shift_copy().start(), lambda: shift_here().start())

    def row_view(ref):
        def view(chunk, part=None):
            first = pl.multiple_of(chunk * rows, 64)
            if part is None:
                return ref.at[pl.ds(first, rows)]
            return ref.at[pl.ds(pl.multiple_of(first + part * (rows // 2), 32), rows // 2)]

        return view

    def prompt_view(chunk, part=None):
        return kvp_v.at[chunk] if part is None else kvp_v.at[chunk, part]

    views = [row_view(wqkv_v), prompt_view, row_view(wo_v)]
    owns = [wqkv_hbm, cache_hbm.at[0], wot_v]
    started = []

    def message(a, kind, chunk, part, to, own=False):
        dst = views[a](chunk, part)
        return pltpu.make_async_remote_copy(
            src_ref=owns[a] if own else dst,
            dst_ref=dst,
            send_sem=g_send.at[a, kind],
            recv_sem=g_recv.at[a, kind],
            device_id=(to, n),
            device_id_type=MESH,
        )

    def send(a, kind, chunk, part, to, own=False):
        message(a, kind, chunk, part, to, own).start()
        started.append((a, kind, chunk, part, to, own))

    def arrived(a, kind, chunk, part=None):
        message(a, kind, chunk, part, w).wait_recv()

    def first(a):
        send(a, 1, w, None, zw, True)
        send(a, 2, w, None, yr, True)
        send(a, 3, w, None, yl, True)
        send(a, 0, w, None, sw, True)

    def second(a):
        arrived(a, 1, zw)
        send(a, 5, zw, None, yr)
        send(a, 6, zw, None, yl)
        send(a, 4, zw, None, sw)

    def third(a):
        arrived(a, 2, yl)
        send(a, 8, yl, 0, yr)
        send(a, 7, yl, None, sw)
        arrived(a, 3, yr)
        send(a, 10, yr, 1, yl)
        send(a, 9, yr, None, sw)

    def fourth(a):
        arrived(a, 5, zl)
        send(a, 12, zl, 0, yr)
        send(a, 11, zl, None, sw)
        arrived(a, 6, zr)
        send(a, 14, zr, 1, yl)
        send(a, 13, zr, None, sw)

    def fifth(a):
        arrived(a, 8, y2, 0)
        arrived(a, 10, y2, 1)
        send(a, 15, y2, None, sw)
        arrived(a, 12, z2, 0)
        arrived(a, 14, z2, 1)
        send(a, 16, z2, None, sw)

    def finish(a):
        for kind, chunk in (
            (0, w), (4, over_z(w)), (7, yl), (9, yr),
            (11, over_z(yl)), (13, over_z(yr)), (15, y2), (16, over_z(y2)),
        ):
            arrived(a, kind, sib(chunk))

    first(0)
    first(1)

    own_half = pl.ds(par * half_layers, half_layers)
    partner_half = pl.ds((1 - par) * half_layers, half_layers)
    own_lanes = pl.ds(half_at, HEAD)

    def z_copy(p):
        at = pl.ds(p * PAIR, PAIR)
        return pltpu.make_async_remote_copy(
            src_ref=zsend_v.at[at], dst_ref=zrecv_v.at[at],
            send_sem=z_send.at[p], recv_sem=z_recv.at[p],
            device_id=(over_z(w), n), device_id_type=MESH,
        )

    def near_x_copy():
        return pltpu.make_async_remote_copy(
            src_ref=xsend_v, dst_ref=ysend_v.at[0, :, :, :, :, own_lanes],
            send_sem=x_send.at[PAIRS], recv_sem=x_recv.at[PAIRS],
            device_id=(w, partner), device_id_type=MESH,
        )

    def far_x_copy(p):
        at = pl.ds(p * PAIR, PAIR)
        return pltpu.make_async_remote_copy(
            src_ref=zrecv_v.at[at, partner_half], dst_ref=ysend_v.at[1, at, :, :, :, own_lanes],
            send_sem=x_send.at[p], recv_sem=x_recv.at[p],
            device_id=(w, partner), device_id_type=MESH,
        )

    def far_own_copy(p):
        at = pl.ds(p * PAIR, PAIR)
        return pltpu.make_async_copy(
            zrecv_v.at[at, own_half], ysend_v.at[1, at, :, :, :, own_lanes], f_sem.at[p]
        )

    def page_for(to):
        page = jnp.int32(0)
        for t in range(WIDE):
            page = jnp.where(route_ref[0, t] == to, jnp.int32(t), page)
        return page

    copies[2].wait()

    def lay_far(d, carry):
        zsend_v[d] = cache_v[:, :, page_for(over_z(plane) + d)]
        return carry

    def lay_near(d, carry):
        page = page_for(plane + d)
        xsend_v[d] = cache_v[partner_half, :, page]
        ysend_v[0, d, :, :, :, own_lanes] = cache_v[own_half, :, page]
        return carry

    lax.fori_loop(0, PLANE, lay_far, 0)
    lax.fori_loop(0, PLANE, lay_near, 0)

    def to_partner(p, carry):
        z_copy(p).wait_recv()
        far_x_copy(p).start()
        far_own_copy(p).start()
        return carry

    tok_id = w * tok_rows + lax.broadcasted_iota(jnp.int32, (tok_rows, HEAD), 0)
    begin = jnp.zeros((tok_rows, HEAD), jnp.int32)
    off = jnp.zeros((tok_rows, HEAD), jnp.int32)
    edge = jnp.int32(0)
    for k in range(REQUESTS):
        inside = tok_id >= edge
        begin = jnp.where(inside, edge, begin)
        off = jnp.where(inside, starts_ref[k] - edge, off)
        edge = edge + lengths_ref[k]
    begin_v[...] = begin
    block_keys = kvp_v.shape[2] * kvp_v.shape[3]
    prompt_len = WIDE * block_keys
    angle = (prompt_len + off + tok_id).astype(F32) * freq_ref[...]
    cos_v[...] = jnp.cos(angle)
    lane = lax.broadcasted_iota(jnp.int32, (tok_rows, HEAD), 1)
    sin_v[...] = jnp.where(lane < HEAD // 2, -1.0, 1.0) * jnp.sin(angle)

    copies[0].wait()
    block = 32

    def norm_block(i, carry):
        at = pl.ds(pl.multiple_of(i * block, block), block)
        xf = x_v[at, :].astype(F32)
        mean = jnp.sum(xf * xf, -1, keepdims=True) * (1.0 / depth)
        x_v[at, :] = (xf * lax.rsqrt(mean + 1e-06) * gain_ref[...]).astype(BF16)
        return carry

    lax.fori_loop(0, tok_rows // block, norm_block, 0)

    either(shifts, lambda: shift_copy().wait_recv(), lambda: shift_here().wait())
    either(turns, lambda: turn_copy().start(), lambda: turn_here().start())
    second(0)
    third(0)
    z_copy(0).start()
    second(1)
    fourth(0)
    third(1)
    z_copy(1).start()
    either(turns, lambda: turn_copy().wait_recv(), lambda: turn_here().wait())
    first(2)
    own_wo2 = pltpu.make_async_copy(wot_v, views[2](w), local_sem.at[5])
    own_wo2.start()
    near_x_copy().start()
    fifth(0)
    finish(0)
    copies[1].wait()
    fourth(1)
    second(2)
    z_copy(2).start()
    z_copy(3).start()

    proj_v[...] = jnp.zeros_like(proj_v)
    step = 1280

    def project(i, carry):
        at = pl.ds(pl.multiple_of(i * step, step), step)
        proj_v[...] += jnp.dot(x_v[:, at], wqkv_v[at, :], preferred_element_type=F32)
        return carry

    lax.fori_loop(0, depth // step, project, 0)

    def rotated(heads, times=1.0):
        turned = heads * cos_v[...] + pltpu.roll(heads, HEAD // 2, 1) * sin_v[...]
        return (turned * times).astype(BF16)

    nkv_v[0, core, 0] = rotated(proj_v[:, GROUP * HEAD : (GROUP + 1) * HEAD])
    nkv_v[0, core, 1] = proj_v[:, (GROUP + 1) * HEAD : (GROUP + 2) * HEAD].astype(BF16)

    def back_copy(kind, slot, slot_to, which, to):
        return pltpu.make_async_remote_copy(
            src_ref=nkv_v.at[slot, which], dst_ref=nkv_v.at[slot_to, which],
            send_sem=n_send.at[kind], recv_sem=n_recv.at[kind],
            device_id=(to, n), device_id_type=MESH,
        )

    back_copies = [
        back_copy(1, 0, 1, core, lax.rem(w + 2, WIDE)),
        back_copy(2, 0, 2, core, lax.rem(w + 4, WIDE)),
        back_copy(0, 0, 0, core, sib(w)),
        back_copy(3, 1, 1, core, sib(w)),
        back_copy(4, 2, 2, core, sib(w)),
    ]
    for copy in back_copies[:3]:
        copy.start()
    factor = HEAD ** (-0.5) * LOG2E
    for h in range(GROUP):
        q_v[h] = rotated(proj_v[:, h * HEAD : (h + 1) * HEAD], factor)

    third(2)
    back_copies[0].wait_recv()
    back_copies[3].start()
    fifth(1)
    back_copies[1].wait_recv()
    back_copies[4].start()
    lax.fori_loop(0, PAIRS // 2, to_partner, 0)

    place = w - plane

    def source_of(s):
        return w if s == 0 else over_z(w)

    def y_copy(s, k, d, source):
        return pltpu.make_async_remote_copy(
            src_ref=ysend_v.at[s, d], dst_ref=relay_ref.at[0, :, :, source],
            send_sem=r_send.at[s, k], recv_sem=r_recv.at[s, k],
            device_id=(plane + d, n), device_id_type=MESH,
        )

    def to_owners(s):
        def step(k, carry):
            y_copy(s, k, lax.rem(place + k, PLANE), source_of(s)).start()
            return carry

        lax.fori_loop(1, PLANE, step, 0)

    def own_page(s):
        return pltpu.make_async_copy(
            ysend_v.at[s, place], relay_ref.at[0, :, :, source_of(s)], o_sem.at[s]
        )

    near_x_copy().wait_recv()
    to_owners(0)
    own_page(0).start()
    finish(1)
    copies[3].wait()
    for kind, slot, copy in ((0, 0, 2), (3, 1, 3), (4, 2, 4)):
        back_copy(kind, slot, slot, 1 - core, sib(w)).wait_recv()

    def scores(h, keys):
        return lax.dot_general(q_v[h], keys, (((1,), (1,)), ((), ())), preferred_element_type=F32)

    def attend(score, vals):
        top = top_v[...]
        new_top = jnp.maximum(top, jnp.max(score, 1, keepdims=True))
        fall = jnp.exp2(top - new_top)
        weight = jnp.exp2(score - new_top[:, :1]).astype(BF16)
        both = jnp.concatenate([vals, jnp.ones(vals.shape, BF16)], 1)
        summed = jnp.dot(weight, both, preferred_element_type=F32)
        acc_v[...] = acc_v[...] * fall + summed[:, :HEAD]
        den_v[...] = den_v[...] * fall + summed[:, HEAD:]
        top_v[...] = new_top

    per_step = KEYS // block_keys
    ring = (n // 4) * 4
    across = lax.rem(n + 4, NARROW)

    def around(k):
        return ring + lax.rem(n + k, 4)

    far_ring = 4 - ring

    def beyond(k):
        return far_ring + lax.rem(n + k, 4)

    lead, trail = around(1), around(3)

    def head_copy(h, kind, owner, to):
        lanes = pl.ds(pl.multiple_of(h * HEAD, HEAD), HEAD)
        if kind < 5:
            at = att_v.at[owner, :, lanes]
        else:
            at = att_v.at[owner, pl.ds((kind + 1) % 2 * (tok_rows // 2), tok_rows // 2), lanes]
        return pltpu.make_async_remote_copy(
            src_ref=at, dst_ref=at, send_sem=a_send.at[h, kind], recv_sem=a_recv.at[h, kind],
            device_id=(w, to), device_id_type=MESH,
        )

    sends = (
        (0, n, lead, trail), (1, n, trail, lead), (2, n, across, across),
        (3, across, lead, beyond(3)), (4, across, trail, beyond(1)),
        (5, trail, lead, around(2)), (6, lead, trail, around(2)),
        (7, beyond(3), lead, beyond(2)), (8, beyond(1), trail, beyond(2)),
    )

    def give(h, *kinds):
        for kind in kinds:
            _, owner, to, _ = sends[kind]
            head_copy(h, kind, owner, to).start()

    def take(h, *kinds):
        for kind in kinds:
            head_copy(h, kind, sends[kind][3], n).wait_recv()

    def pass_on(h):
        take(h, 2)
        give(h, 3, 4)
        take(h, 0)
        give(h, 5)
        take(h, 1)
        give(h, 6)

    def pass_further(h):
        take(h, 3)
        give(h, 7)
        take(h, 4)
        give(h, 8)

    def head_step(h, carry):
        top_v[...] = jnp.full_like(top_v, -1e30)
        den_v[...] = jnp.zeros_like(den_v)
        acc_v[...] = jnp.zeros_like(acc_v)

        steps = WIDE // per_step

        def keys_at(i):
            return kvp_v[i * per_step : (i + 1) * per_step, 0].reshape(KEYS, HEAD)

        def vals_at(i):
            return kvp_v[i * per_step : (i + 1) * per_step, 1].reshape(KEYS, HEAD)

        slots = []
        for j in range(BACK + 1):
            source = lax.rem(w - j + WIDE, WIDE)
            slots.append((lax.rem(w // 2 - source // 2 + PLANE, PLANE), lax.rem(source, 2)))
        new_keys = jnp.concatenate([nkv_v[away, which, 0] for away, which in slots], 0)
        new_vals = jnp.concatenate([nkv_v[away, which, 1] for away, which in slots], 0)
        ahead = scores(h, keys_at(0))
        for i in range(steps):
            score = ahead
            ahead = scores(h, keys_at(i + 1) if i + 1 < steps else new_keys)
            attend(score, vals_at(i))
        score = ahead
        own_id = w * tok_rows + lax.broadcasted_iota(jnp.int32, (tok_rows, tok_rows), 0)
        masked = []
        for j in range(BACK + 1):
            key_id = (w - j) * tok_rows + lax.broadcasted_iota(jnp.int32, (tok_rows, tok_rows), 1)
            visible = key_id >= begin_v[:, :1]
            if j == 0:
                visible = visible & (key_id <= own_id)
            masked.append(jnp.where(visible, score[:, j * tok_rows : (j + 1) * tok_rows], -1e30))
        attend(jnp.concatenate(masked, 1), new_vals)
        att_v[n, :, pl.ds(pl.multiple_of(h * HEAD, HEAD), HEAD)] = (acc_v[...] / den_v[...]).astype(BF16)
        give(h, 2, 0, 1)

        @pl.when(h == 0)
        def _():
            fourth(2)
            lax.fori_loop(PAIRS // 2, PAIRS, to_partner, 0)

        @pl.when(h == 1)
        def _():
            fifth(2)

            def far_ready(p, inner):
                far_x_copy(p).wait_recv()
                far_own_copy(p).wait()
                return inner

            lax.fori_loop(0, PAIRS, far_ready, 0)
            to_owners(1)
            own_page(1).start()

        @pl.when(h > 0)
        def _():
            pass_on(h - 1)

        @pl.when(h > 1)
        def _():
            pass_further(h - 2)

        return carry

    lax.fori_loop(0, GROUP, head_step, 0)
    last = GROUP - 1
    pass_further(last - 1)
    pass_on(last)

    finish(2)
    own_wo2.wait()
    out_v[...] = jnp.zeros_like(out_v)
    span = out_v.shape[1]

    early = last * HEAD

    def earlier(h, carry):
        take(h, 5, 6, 7, 8)
        return carry

    lax.fori_loop(0, last, earlier, 0)

    def out_step(owner, carry, at=0, size=early):
        held = mix(owner // 4, z_at) * 4 + lax.rem(owner + x_at, 4)
        rows_at = pl.ds(pl.multiple_of(held * span, span), span)
        out_v[...] += lax.dot_general(
            att_v[owner, :, at : at + size], wo_v[rows_at, at : at + size],
            (((1,), (1,)), ((), ())), preferred_element_type=F32,
        )
        return carry

    lax.fori_loop(0, NARROW // 2, out_step, 0)
    pass_further(last)
    lax.fori_loop(NARROW // 2, NARROW, out_step, 0)
    take(last, 5, 6, 7, 8)
    lax.fori_loop(0, NARROW, lambda owner, carry: out_step(owner, carry, early, HEAD), 0)
    out_ref[...] = out_v[...].astype(BF16)

    def sent(h, carry):
        for kind, owner, to, _ in sends:
            head_copy(h, kind, owner, to).wait_send()
        return carry

    lax.fori_loop(0, GROUP, sent, 0)
    for sending in started:
        message(*sending).wait_send()
    for copy in back_copies:
        copy.wait_send()

    either(shifts, lambda: shift_copy().wait_send(), lambda: None)
    either(turns, lambda: turn_copy().wait_send(), lambda: None)

    def far_sent(p, carry):
        z_copy(p).wait_send()
        far_x_copy(p).wait_send()
        return carry

    lax.fori_loop(0, PAIRS, far_sent, 0)
    near_x_copy().wait_send()
    for s in range(2):
        own_page(s).wait()

        def relay_end(k, carry):
            y_copy(s, k, lax.rem(place + k, PLANE), source_of(s)).wait_send()
            giver = plane + lax.rem(place - k + PLANE, PLANE)
            y_copy(s, k, place, giver if s == 0 else over_z(giver)).wait_recv()
            return carry

        lax.fori_loop(1, PLANE, relay_end, 0)


def on_device(
    tokens,
    norm_gain,
    w_query,
    w_keyval,
    w_output,
    prompt_cache,
    stretch_lengths,
    stretch_starts,
    page_route,
):
    tok_rows, depth = tokens.shape
    rows, q_cols = w_query.shape
    layers, kinds, cache_rows, channels = prompt_cache.shape
    pages = page_route.shape[1]
    page_rows = cache_rows // pages
    half = layers // 2
    cols = q_cols + 2 * channels
    wqkv = jnp.concatenate([w_query, w_keyval.reshape(rows, 2 * channels)], 1)
    freq = 1000000.0 ** (-jnp.arange(HEAD // 2, dtype=jnp.float32) * 2.0 / HEAD)
    freq = jnp.concatenate([freq, freq])[None]
    any_spec = pl.BlockSpec(memory_space=pl.ANY)
    vmem_spec = pl.BlockSpec(memory_space=pltpu.VMEM)
    smem_spec = pl.BlockSpec(memory_space=pltpu.SMEM)
    cache5 = prompt_cache.reshape(layers, kinds, pages, page_rows, channels)
    dma = pltpu.SemaphoreType.DMA
    attn_out, relay = pl.pallas_call(
        whole_kernel,
        out_shape=(
            jax.ShapeDtypeStruct((tok_rows, q_cols), BF16),
            jax.ShapeDtypeStruct((1, half, kinds, WIDE, page_rows, 2 * channels), BF16),
        ),
        in_specs=[
            any_spec, vmem_spec, any_spec, any_spec, any_spec, vmem_spec,
            smem_spec, smem_spec, smem_spec,
        ],
        out_specs=(vmem_spec, any_spec),
        scratch_shapes=[
            pltpu.VMEM((tok_rows, depth), BF16),
            pltpu.VMEM((WIDE * rows, cols), BF16),
            pltpu.VMEM((WIDE, kinds, pages, page_rows, channels), BF16),
            pltpu.VMEM((rows, q_cols), BF16),
            pltpu.VMEM((rows, q_cols), BF16),
            pltpu.VMEM((WIDE * rows, q_cols), BF16),
            pltpu.VMEM((layers, kinds, pages, page_rows, channels), BF16),
            pltpu.VMEM((PLANE, layers, kinds, page_rows, channels), BF16),
            pltpu.VMEM((PLANE, layers, kinds, page_rows, channels), BF16),
            pltpu.VMEM((PLANE, half, kinds, page_rows, channels), BF16),
            pltpu.VMEM((2, PLANE, half, kinds, page_rows, 2 * channels), BF16),
            pltpu.VMEM((tok_rows, cols), F32),
            pltpu.VMEM((GROUP, tok_rows, HEAD), BF16),
            pltpu.VMEM((3, 2, 2, tok_rows, HEAD), BF16),
            pltpu.VMEM((NARROW, tok_rows, q_cols), BF16),
            pltpu.VMEM((tok_rows, HEAD), F32),
            pltpu.VMEM((tok_rows, HEAD), F32),
            pltpu.VMEM((tok_rows, HEAD), F32),
            pltpu.VMEM((tok_rows, HEAD), F32),
            pltpu.VMEM((tok_rows, HEAD), F32),
            pltpu.VMEM((tok_rows, HEAD), jnp.int32),
            pltpu.VMEM((tok_rows, q_cols), F32),
            dma((7,)),
            dma((3, MESSAGES)),
            dma((3, MESSAGES)),
            dma((2,)),
            dma((2,)),
            dma((PAIRS + 1,)),
            dma((PAIRS + 1,)),
            dma((PAIRS,)),
            dma((PAIRS,)),
            dma((PAIRS,)),
            dma((2,)),
            dma((2, PLANE)),
            dma((2, PLANE)),
            dma((5,)),
            dma((5,)),
            dma((GROUP, 9)),
            dma((GROUP, 9)),
        ],
        compiler_params=pltpu.CompilerParams(
            collective_id=0, has_side_effects=True, vmem_limit_bytes=60 * 2**20
        ),
    )(
        tokens, norm_gain[None], wqkv, w_output.T, cache5, freq,
        stretch_lengths, stretch_starts, page_route,
    )
    return attn_out, relay


def solution(mesh):
    placed = (
        P("wide", None),
        P(),
        P("wide", "narrow"),
        P("wide", None, "narrow"),
        P("narrow", "wide"),
        P(None, None, "wide", "narrow"),
        P(),
        P(),
        P("wide", None),
    )
    return jax.shard_map(
        on_device,
        mesh=mesh,
        in_specs=placed,
        out_specs=(P("wide", "narrow"), P("narrow", None, None, "wide", None, None)),
        check_vma=False,
    )
```

```python
import functools

import jax
import jax.numpy as jnp
import numpy as np
from jax import lax
from jax.experimental import pallas as pl
from jax.experimental.pallas import tpu as pltpu
from jax.sharding import PartitionSpec as P

MESH = pl.DeviceIdType.MESH
HEAD = 128
GROUP = 5
REQUESTS = 16
WIDE = 16
NARROW = 8
BF16 = jnp.bfloat16
F32 = jnp.float32
KEYS = 2048
BACK = 4
LOG2E = 1.4426950408889634
MESSAGES = 17
PLANE = 8
PAIR = 2
PAIRS = PLANE // PAIR


def whole_kernel(
    tok_hbm,
    gain_ref,
    wq_hbm,
    wkv_hbm,
    wo_hbm,
    cache_hbm,
    freq_ref,
    lengths_ref,
    starts_ref,
    route_ref,
    out_ref,
    relay_ref,
    x_v,
    wqkv_v,
    kvp_v,
    wos_v,
    wot_v,
    wo_v,
    cache_v,
    zsend_v,
    zrecv_v,
    xsend_v,
    ysend_v,
    proj_v,
    q_v,
    nkv_v,
    att_v,
    acc_v,
    top_v,
    den_v,
    cos_v,
    sin_v,
    begin_v,
    out_v,
    local_sem,
    g_send,
    g_recv,
    t_send,
    t_recv,
    x_send,
    x_recv,
    z_send,
    z_recv,
    f_sem,
    o_sem,
    r_send,
    r_recv,
    n_send,
    n_recv,
    a_send,
    a_recv,
):
    tok_rows, depth = x_v.shape
    rows, q_cols = wq_hbm.shape
    own_rows = pl.ds(pl.multiple_of(lax.axis_index("wide") * rows, 64), rows)
    half_layers = xsend_v.shape[1]
    w = lax.axis_index("wide")
    n = lax.axis_index("narrow")
    core = lax.rem(w, 2)
    y = lax.rem(w // 2, 4)
    zh = w // 8
    plane = zh * 8

    def at_y(step):
        return plane + lax.rem(y + step, 4) * 2 + core

    def sib(chunk):
        return chunk + 1 - 2 * core

    def over_z(chunk):
        return lax.rem(chunk + 8, 16)

    yr, yl, y2 = at_y(1), at_y(3), at_y(2)
    zw, zr, zl, z2 = over_z(w), over_z(yr), over_z(yl), over_z(y2)
    sw = sib(w)
    par = lax.rem(n, 2)
    partner = n + 1 - 2 * par
    x_at, z_at = lax.rem(n, 4), n // 4

    def mix(one, other):
        return one + other - 2 * one * other

    shift_w = mix(zh, z_at) * 8 + lax.rem(y + x_at, 4) * 2 + core
    shifts = n > 0
    turn_n = mix(zh, z_at) * 4 + lax.rem(y - x_at + 4, 4)
    turns = turn_n != n

    half_at = pl.multiple_of(par * HEAD, HEAD)
    copies = [
        pltpu.make_async_copy(tok_hbm, x_v, local_sem.at[0]),
        pltpu.make_async_copy(wq_hbm, wqkv_v.at[own_rows, pl.ds(0, q_cols)], local_sem.at[1]),
        pltpu.make_async_copy(cache_hbm, cache_v, local_sem.at[2]),
        pltpu.make_async_copy(cache_hbm.at[0], kvp_v.at[w], local_sem.at[3]),
        pltpu.make_async_copy(
            wkv_hbm, wqkv_v.at[own_rows, pl.ds(q_cols, wkv_hbm.shape[1])], local_sem.at[7]
        ),
    ]
    for copy in copies:
        copy.start()

    barrier = pltpu.get_barrier_semaphore()

    def greet_wide(k, carry):
        pl.semaphore_signal(barrier, inc=1, device_id=(lax.rem(w + k, WIDE), n), device_id_type=MESH)
        return carry

    def greet_narrow(k, carry):
        pl.semaphore_signal(barrier, inc=1, device_id=(w, lax.rem(n + k, NARROW)), device_id_type=MESH)
        return carry

    lax.fori_loop(1, WIDE, greet_wide, 0)
    lax.fori_loop(1, NARROW, greet_narrow, 0)

    pl.semaphore_wait(barrier, WIDE - 1 + NARROW - 1)

    def shift_copy():
        return pltpu.make_async_remote_copy(
            src_ref=wo_hbm, dst_ref=wos_v, send_sem=t_send.at[0], recv_sem=t_recv.at[0],
            device_id=(shift_w, n), device_id_type=MESH,
        )

    def turn_copy():
        return pltpu.make_async_remote_copy(
            src_ref=wos_v, dst_ref=wot_v, send_sem=t_send.at[1], recv_sem=t_recv.at[1],
            device_id=(w, turn_n), device_id_type=MESH,
        )

    def shift_here():
        return pltpu.make_async_copy(wo_hbm, wos_v, local_sem.at[4])

    def turn_here():
        return pltpu.make_async_copy(wos_v, wot_v, local_sem.at[6])

    def either(moves, far, here):
        @pl.when(moves)
        def _():
            far()

        @pl.when(jnp.logical_not(moves))
        def _():
            here()

    either(shifts, lambda: shift_copy().start(), lambda: shift_here().start())

    def row_view(ref):
        def view(chunk, part=None):
            first = pl.multiple_of(chunk * rows, 64)
            if part is None:
                return ref.at[pl.ds(first, rows)]
            return ref.at[pl.ds(pl.multiple_of(first + part * (rows // 2), 32), rows // 2)]

        return view

    def prompt_view(chunk, part=None):
        return kvp_v.at[chunk] if part is None else kvp_v.at[chunk, part]

    views = [row_view(wqkv_v), prompt_view, row_view(wo_v)]
    owns = [None, cache_hbm.at[0], wot_v]
    started = []

    def message(a, kind, chunk, part, to, own=False):
        dst = views[a](chunk, part)
        return pltpu.make_async_remote_copy(
            src_ref=owns[a] if own and a > 0 else dst,
            dst_ref=dst,
            send_sem=g_send.at[a, kind],
            recv_sem=g_recv.at[a, kind],
            device_id=(to, n),
            device_id_type=MESH,
        )

    def send(a, kind, chunk, part, to, own=False):
        message(a, kind, chunk, part, to, own).start()
        started.append((a, kind, chunk, part, to, own))

    def arrived(a, kind, chunk, part=None):
        message(a, kind, chunk, part, w).wait_recv()

    def first(a):
        send(a, 1, w, None, zw, True)
        send(a, 2, w, None, yr, True)
        send(a, 3, w, None, yl, True)
        send(a, 0, w, None, sw, True)

    def second(a):
        arrived(a, 1, zw)
        send(a, 5, zw, None, yr)
        send(a, 6, zw, None, yl)
        send(a, 4, zw, None, sw)

    def third(a):
        arrived(a, 2, yl)
        send(a, 8, yl, 0, yr)
        send(a, 7, yl, None, sw)
        arrived(a, 3, yr)
        send(a, 10, yr, 1, yl)
        send(a, 9, yr, None, sw)

    def fourth(a):
        arrived(a, 5, zl)
        send(a, 12, zl, 0, yr)
        send(a, 11, zl, None, sw)
        arrived(a, 6, zr)
        send(a, 14, zr, 1, yl)
        send(a, 13, zr, None, sw)

    def fifth(a):
        arrived(a, 8, y2, 0)
        arrived(a, 10, y2, 1)
        send(a, 15, y2, None, sw)
        arrived(a, 12, z2, 0)
        arrived(a, 14, z2, 1)
        send(a, 16, z2, None, sw)

    def finish(a):
        for kind, chunk in (
            (0, w), (4, over_z(w)), (7, yl), (9, yr),
            (11, over_z(yl)), (13, over_z(yr)), (15, y2), (16, over_z(y2)),
        ):
            arrived(a, kind, sib(chunk))

    copies[1].wait()
    copies[4].wait()
    first(0)
    first(1)

    own_half = pl.ds(par * half_layers, half_layers)
    partner_half = pl.ds((1 - par) * half_layers, half_layers)
    own_lanes = pl.ds(half_at, HEAD)

    def z_copy(p):
        at = pl.ds(p * PAIR, PAIR)
        return pltpu.make_async_remote_copy(
            src_ref=zsend_v.at[at], dst_ref=zrecv_v.at[at],
            send_sem=z_send.at[p], recv_sem=z_recv.at[p],
            device_id=(over_z(w), n), device_id_type=MESH,
        )

    def near_x_copy():
        return pltpu.make_async_remote_copy(
            src_ref=xsend_v, dst_ref=ysend_v.at[0, :, :, :, :, own_lanes],
            send_sem=x_send.at[PAIRS], recv_sem=x_recv.at[PAIRS],
            device_id=(w, partner), device_id_type=MESH,
        )

    def far_x_copy(p):
        at = pl.ds(p * PAIR, PAIR)
        return pltpu.make_async_remote_copy(
            src_ref=zrecv_v.at[at, partner_half], dst_ref=ysend_v.at[1, at, :, :, :, own_lanes],
            send_sem=x_send.at[p], recv_sem=x_recv.at[p],
            device_id=(w, partner), device_id_type=MESH,
        )

    def far_own_copy(p):
        at = pl.ds(p * PAIR, PAIR)
        return pltpu.make_async_copy(
            zrecv_v.at[at, own_half], ysend_v.at[1, at, :, :, :, own_lanes], f_sem.at[p]
        )

    def page_for(to):
        page = jnp.int32(0)
        for t in range(WIDE):
            page = jnp.where(route_ref[0, t] == to, jnp.int32(t), page)
        return page

    copies[2].wait()

    def lay_far(d, carry):
        zsend_v[d] = cache_v[:, :, page_for(over_z(plane) + d)]
        return carry

    def lay_near(d, carry):
        page = page_for(plane + d)
        xsend_v[d] = cache_v[partner_half, :, page]
        ysend_v[0, d, :, :, :, own_lanes] = cache_v[own_half, :, page]
        return carry

    lax.fori_loop(0, PLANE, lay_far, 0)
    lax.fori_loop(0, PLANE, lay_near, 0)

    def to_partner(p, carry):
        z_copy(p).wait_recv()
        far_x_copy(p).start()
        far_own_copy(p).start()
        return carry

    tok_id = w * tok_rows + lax.broadcasted_iota(jnp.int32, (tok_rows, HEAD), 0)
    begin = jnp.zeros((tok_rows, HEAD), jnp.int32)
    off = jnp.zeros((tok_rows, HEAD), jnp.int32)
    edge = jnp.int32(0)
    for k in range(REQUESTS):
        inside = tok_id >= edge
        begin = jnp.where(inside, edge, begin)
        off = jnp.where(inside, starts_ref[k] - edge, off)
        edge = edge + lengths_ref[k]
    begin_v[...] = begin
    block_keys = kvp_v.shape[2] * kvp_v.shape[3]
    prompt_len = WIDE * block_keys
    angle = (prompt_len + off + tok_id).astype(F32) * freq_ref[...]
    cos_v[...] = jnp.cos(angle)
    lane = lax.broadcasted_iota(jnp.int32, (tok_rows, HEAD), 1)
    sin_v[...] = jnp.where(lane < HEAD // 2, -1.0, 1.0) * jnp.sin(angle)

    copies[0].wait()
    block = 32

    def norm_block(i, carry):
        at = pl.ds(pl.multiple_of(i * block, block), block)
        xf = x_v[at, :].astype(F32)
        mean = jnp.sum(xf * xf, -1, keepdims=True) * (1.0 / depth)
        x_v[at, :] = (xf * lax.rsqrt(mean + 1e-06) * gain_ref[...]).astype(BF16)
        return carry

    lax.fori_loop(0, tok_rows // block, norm_block, 0)

    either(shifts, lambda: shift_copy().wait_recv(), lambda: shift_here().wait())
    either(turns, lambda: turn_copy().start(), lambda: turn_here().start())
    second(0)
    third(0)
    z_copy(0).start()
    second(1)
    fourth(0)
    third(1)
    z_copy(1).start()
    either(turns, lambda: turn_copy().wait_recv(), lambda: turn_here().wait())
    first(2)
    own_wo2 = pltpu.make_async_copy(wot_v, views[2](w), local_sem.at[5])
    own_wo2.start()
    near_x_copy().start()
    fifth(0)
    finish(0)
    fourth(1)
    second(2)
    z_copy(2).start()
    z_copy(3).start()

    proj_v[...] = jnp.zeros_like(proj_v)
    step = 1280

    def project(i, carry):
        at = pl.ds(pl.multiple_of(i * step, step), step)
        proj_v[...] += jnp.dot(x_v[:, at], wqkv_v[at, :], preferred_element_type=F32)
        return carry

    lax.fori_loop(0, depth // step, project, 0)

    def rotated(heads, times=1.0):
        turned = heads * cos_v[...] + pltpu.roll(heads, HEAD // 2, 1) * sin_v[...]
        return (turned * times).astype(BF16)

    nkv_v[0, core, 0] = rotated(proj_v[:, GROUP * HEAD : (GROUP + 1) * HEAD])
    nkv_v[0, core, 1] = proj_v[:, (GROUP + 1) * HEAD : (GROUP + 2) * HEAD].astype(BF16)

    def back_copy(kind, slot, slot_to, which, to):
        return pltpu.make_async_remote_copy(
            src_ref=nkv_v.at[slot, which], dst_ref=nkv_v.at[slot_to, which],
            send_sem=n_send.at[kind], recv_sem=n_recv.at[kind],
            device_id=(to, n), device_id_type=MESH,
        )

    back_copies = [
        back_copy(1, 0, 1, core, lax.rem(w + 2, WIDE)),
        back_copy(2, 0, 2, core, lax.rem(w + 4, WIDE)),
        back_copy(0, 0, 0, core, sib(w)),
        back_copy(3, 1, 1, core, sib(w)),
        back_copy(4, 2, 2, core, sib(w)),
    ]
    for copy in back_copies[:3]:
        copy.start()
    factor = HEAD ** (-0.5) * LOG2E
    for h in range(GROUP):
        q_v[h] = rotated(proj_v[:, h * HEAD : (h + 1) * HEAD], factor)

    third(2)
    back_copies[0].wait_recv()
    back_copies[3].start()
    fifth(1)
    back_copies[1].wait_recv()
    back_copies[4].start()
    lax.fori_loop(0, PAIRS // 2, to_partner, 0)

    place = w - plane

    def source_of(s):
        return w if s == 0 else over_z(w)

    def y_copy(s, k, d, source):
        return pltpu.make_async_remote_copy(
            src_ref=ysend_v.at[s, d], dst_ref=relay_ref.at[0, :, :, source],
            send_sem=r_send.at[s, k], recv_sem=r_recv.at[s, k],
            device_id=(plane + d, n), device_id_type=MESH,
        )

    def to_owners(s):
        def step(k, carry):
            y_copy(s, k, lax.rem(place + k, PLANE), source_of(s)).start()
            return carry

        lax.fori_loop(1, PLANE, step, 0)

    def own_page(s):
        return pltpu.make_async_copy(
            ysend_v.at[s, place], relay_ref.at[0, :, :, source_of(s)], o_sem.at[s]
        )

    near_x_copy().wait_recv()
    to_owners(0)
    own_page(0).start()
    finish(1)
    copies[3].wait()
    for kind, slot, copy in ((0, 0, 2), (3, 1, 3), (4, 2, 4)):
        back_copy(kind, slot, slot, 1 - core, sib(w)).wait_recv()

    def scores(h, keys):
        return lax.dot_general(q_v[h], keys, (((1,), (1,)), ((), ())), preferred_element_type=F32)

    def attend(score, vals):
        top = top_v[...]
        new_top = jnp.maximum(top, jnp.max(score, 1, keepdims=True))
        fall = jnp.exp2(top - new_top)
        weight = jnp.exp2(score - new_top[:, :1]).astype(BF16)
        both = jnp.concatenate([vals, jnp.ones(vals.shape, BF16)], 1)
        summed = jnp.dot(weight, both, preferred_element_type=F32)
        acc_v[...] = acc_v[...] * fall + summed[:, :HEAD]
        den_v[...] = den_v[...] * fall + summed[:, HEAD:]
        top_v[...] = new_top

    per_step = KEYS // block_keys
    ring = (n // 4) * 4
    across = lax.rem(n + 4, NARROW)

    def around(k):
        return ring + lax.rem(n + k, 4)

    far_ring = 4 - ring

    def beyond(k):
        return far_ring + lax.rem(n + k, 4)

    lead, trail = around(1), around(3)

    def head_copy(h, kind, owner, to):
        lanes = pl.ds(pl.multiple_of(h * HEAD, HEAD), HEAD)
        if kind < 5:
            at = att_v.at[owner, :, lanes]
        else:
            at = att_v.at[owner, pl.ds((kind + 1) % 2 * (tok_rows // 2), tok_rows // 2), lanes]
        return pltpu.make_async_remote_copy(
            src_ref=at, dst_ref=at, send_sem=a_send.at[h, kind], recv_sem=a_recv.at[h, kind],
            device_id=(w, to), device_id_type=MESH,
        )

    sends = (
        (0, n, lead, trail), (1, n, trail, lead), (2, n, across, across),
        (3, across, lead, beyond(3)), (4, across, trail, beyond(1)),
        (5, trail, lead, around(2)), (6, lead, trail, around(2)),
        (7, beyond(3), lead, beyond(2)), (8, beyond(1), trail, beyond(2)),
    )

    def give(h, *kinds):
        for kind in kinds:
            _, owner, to, _ = sends[kind]
            head_copy(h, kind, owner, to).start()

    def take(h, *kinds):
        for kind in kinds:
            head_copy(h, kind, sends[kind][3], n).wait_recv()

    def pass_on(h):
        take(h, 2)
        give(h, 3, 4)
        take(h, 0)
        give(h, 5)
        take(h, 1)
        give(h, 6)

    def pass_further(h):
        take(h, 3)
        give(h, 7)
        take(h, 4)
        give(h, 8)

    def head_step(h, carry):
        top_v[...] = jnp.full_like(top_v, -1e30)
        den_v[...] = jnp.zeros_like(den_v)
        acc_v[...] = jnp.zeros_like(acc_v)

        steps = WIDE // per_step

        def keys_at(i):
            return kvp_v[i * per_step : (i + 1) * per_step, 0].reshape(KEYS, HEAD)

        def vals_at(i):
            return kvp_v[i * per_step : (i + 1) * per_step, 1].reshape(KEYS, HEAD)

        slots = []
        for j in range(BACK + 1):
            source = lax.rem(w - j + WIDE, WIDE)
            slots.append((lax.rem(w // 2 - source // 2 + PLANE, PLANE), lax.rem(source, 2)))
        new_keys = jnp.concatenate([nkv_v[away, which, 0] for away, which in slots], 0)
        new_vals = jnp.concatenate([nkv_v[away, which, 1] for away, which in slots], 0)
        ahead = scores(h, keys_at(0))
        for i in range(steps):
            score = ahead
            ahead = scores(h, keys_at(i + 1) if i + 1 < steps else new_keys)
            attend(score, vals_at(i))
        score = ahead
        own_id = w * tok_rows + lax.broadcasted_iota(jnp.int32, (tok_rows, tok_rows), 0)
        masked = []
        for j in range(BACK + 1):
            key_id = (w - j) * tok_rows + lax.broadcasted_iota(jnp.int32, (tok_rows, tok_rows), 1)
            visible = key_id >= begin_v[:, :1]
            if j == 0:
                visible = visible & (key_id <= own_id)
            masked.append(jnp.where(visible, score[:, j * tok_rows : (j + 1) * tok_rows], -1e30))
        attend(jnp.concatenate(masked, 1), new_vals)
        att_v[n, :, pl.ds(pl.multiple_of(h * HEAD, HEAD), HEAD)] = (acc_v[...] / den_v[...]).astype(BF16)
        give(h, 2, 0, 1)

        @pl.when(h > 0)
        def _():
            pass_on(h - 1)

        @pl.when(h > 1)
        def _():
            pass_further(h - 2)

        @pl.when(h == 0)
        def _():
            fourth(2)
            lax.fori_loop(PAIRS // 2, PAIRS, to_partner, 0)

        @pl.when(h == 3)
        def _():
            fifth(2)

            def far_ready(p, inner):
                far_x_copy(p).wait_recv()
                far_own_copy(p).wait()
                return inner

            lax.fori_loop(0, PAIRS, far_ready, 0)
            to_owners(1)
            own_page(1).start()

        return carry

    lax.fori_loop(0, GROUP, head_step, 0)
    last = GROUP - 1
    pass_further(last - 1)
    pass_on(last)

    finish(2)
    own_wo2.wait()
    out_v[...] = jnp.zeros_like(out_v)
    span = out_v.shape[1]

    early = last * HEAD

    def earlier(h, carry):
        take(h, 5, 6, 7, 8)
        return carry

    lax.fori_loop(0, last, earlier, 0)

    def out_step(owner, carry, at=0, size=early):
        held = mix(owner // 4, z_at) * 4 + lax.rem(owner + x_at, 4)
        rows_at = pl.ds(pl.multiple_of(held * span, span), span)
        out_v[...] += lax.dot_general(
            att_v[owner, :, at : at + size], wo_v[rows_at, at : at + size],
            (((1,), (1,)), ((), ())), preferred_element_type=F32,
        )
        return carry

    lax.fori_loop(0, NARROW // 2, out_step, 0)
    pass_further(last)
    lax.fori_loop(NARROW // 2, NARROW, out_step, 0)
    take(last, 5, 6, 7, 8)
    lax.fori_loop(0, NARROW, lambda owner, carry: out_step(owner, carry, early, HEAD), 0)
    out_ref[...] = out_v[...].astype(BF16)

    def sent(h, carry):
        for kind, owner, to, _ in sends:
            head_copy(h, kind, owner, to).wait_send()
        return carry

    lax.fori_loop(0, GROUP, sent, 0)
    for sending in started:
        message(*sending).wait_send()
    for copy in back_copies:
        copy.wait_send()

    either(shifts, lambda: shift_copy().wait_send(), lambda: None)
    either(turns, lambda: turn_copy().wait_send(), lambda: None)

    def far_sent(p, carry):
        z_copy(p).wait_send()
        far_x_copy(p).wait_send()
        return carry

    lax.fori_loop(0, PAIRS, far_sent, 0)
    near_x_copy().wait_send()
    for s in range(2):
        own_page(s).wait()

        def relay_end(k, carry):
            y_copy(s, k, lax.rem(place + k, PLANE), source_of(s)).wait_send()
            giver = plane + lax.rem(place - k + PLANE, PLANE)
            y_copy(s, k, place, giver if s == 0 else over_z(giver)).wait_recv()
            return carry

        lax.fori_loop(1, PLANE, relay_end, 0)


def on_device(
    tokens,
    norm_gain,
    w_query,
    w_keyval,
    w_output,
    prompt_cache,
    stretch_lengths,
    stretch_starts,
    page_route,
):
    tok_rows, depth = tokens.shape
    rows, q_cols = w_query.shape
    layers, kinds, cache_rows, channels = prompt_cache.shape
    pages = page_route.shape[1]
    page_rows = cache_rows // pages
    half = layers // 2
    cols = q_cols + 2 * channels
    freq = 1000000.0 ** (-np.arange(HEAD // 2) * 2.0 / HEAD)
    freq = jnp.asarray(np.concatenate([freq, freq])[None], jnp.float32)
    any_spec = pl.BlockSpec(memory_space=pl.ANY)
    vmem_spec = pl.BlockSpec(memory_space=pltpu.VMEM)
    smem_spec = pl.BlockSpec(memory_space=pltpu.SMEM)
    cache5 = prompt_cache.reshape(layers, kinds, pages, page_rows, channels)
    dma = pltpu.SemaphoreType.DMA
    attn_out, relay = pl.pallas_call(
        whole_kernel,
        out_shape=(
            jax.ShapeDtypeStruct((tok_rows, q_cols), BF16),
            jax.ShapeDtypeStruct((1, half, kinds, WIDE, page_rows, 2 * channels), BF16),
        ),
        in_specs=[
            any_spec, vmem_spec, any_spec, any_spec, any_spec, any_spec, vmem_spec,
            smem_spec, smem_spec, smem_spec,
        ],
        out_specs=(vmem_spec, any_spec),
        scratch_shapes=[
            pltpu.VMEM((tok_rows, depth), BF16),
            pltpu.VMEM((WIDE * rows, cols), BF16),
            pltpu.VMEM((WIDE, kinds, pages, page_rows, channels), BF16),
            pltpu.VMEM((rows, q_cols), BF16),
            pltpu.VMEM((rows, q_cols), BF16),
            pltpu.VMEM((WIDE * rows, q_cols), BF16),
            pltpu.VMEM((layers, kinds, pages, page_rows, channels), BF16),
            pltpu.VMEM((PLANE, layers, kinds, page_rows, channels), BF16),
            pltpu.VMEM((PLANE, layers, kinds, page_rows, channels), BF16),
            pltpu.VMEM((PLANE, half, kinds, page_rows, channels), BF16),
            pltpu.VMEM((2, PLANE, half, kinds, page_rows, 2 * channels), BF16),
            pltpu.VMEM((tok_rows, cols), F32),
            pltpu.VMEM((GROUP, tok_rows, HEAD), BF16),
            pltpu.VMEM((3, 2, 2, tok_rows, HEAD), BF16),
            pltpu.VMEM((NARROW, tok_rows, q_cols), BF16),
            pltpu.VMEM((tok_rows, HEAD), F32),
            pltpu.VMEM((tok_rows, HEAD), F32),
            pltpu.VMEM((tok_rows, HEAD), F32),
            pltpu.VMEM((tok_rows, HEAD), F32),
            pltpu.VMEM((tok_rows, HEAD), F32),
            pltpu.VMEM((tok_rows, HEAD), jnp.int32),
            pltpu.VMEM((tok_rows, q_cols), F32),
            dma((8,)),
            dma((3, MESSAGES)),
            dma((3, MESSAGES)),
            dma((2,)),
            dma((2,)),
            dma((PAIRS + 1,)),
            dma((PAIRS + 1,)),
            dma((PAIRS,)),
            dma((PAIRS,)),
            dma((PAIRS,)),
            dma((2,)),
            dma((2, PLANE)),
            dma((2, PLANE)),
            dma((5,)),
            dma((5,)),
            dma((GROUP, 9)),
            dma((GROUP, 9)),
        ],
        compiler_params=pltpu.CompilerParams(
            collective_id=0, has_side_effects=True, vmem_limit_bytes=60 * 2**20
        ),
    )(
        tokens, norm_gain[None], w_query, w_keyval.reshape(rows, 2 * channels), w_output.T, cache5, freq,
        stretch_lengths, stretch_starts, page_route,
    )
    return attn_out, relay


def solution(mesh):
    placed = (
        P("wide", None),
        P(),
        P("wide", "narrow"),
        P("wide", None, "narrow"),
        P("narrow", "wide"),
        P(None, None, "wide", "narrow"),
        P(),
        P(),
        P("wide", None),
    )
    return jax.shard_map(
        on_device,
        mesh=mesh,
        in_specs=placed,
        out_specs=(P("wide", "narrow"), P("narrow", None, None, "wide", None, None)),
        check_vma=False,
    )
```

```python
import functools

import jax
import jax.numpy as jnp
import numpy as np
from jax import lax
from jax.experimental import pallas as pl
from jax.experimental.pallas import tpu as pltpu
from jax.sharding import PartitionSpec as P

MESH = pl.DeviceIdType.MESH
HEAD = 128
GROUP = 5
REQUESTS = 16
WIDE = 16
NARROW = 8
BF16 = jnp.bfloat16
F32 = jnp.float32
KEYS = 2048
BACK = 4
LOG2E = 1.4426950408889634
MESSAGES = 17
PLANE = 8
PAIR = 2
PAIRS = PLANE // PAIR


def whole_kernel(
    tok_hbm,
    gain_ref,
    wq_hbm,
    wkv_hbm,
    wo_hbm,
    cache_hbm,
    freq_ref,
    lengths_ref,
    starts_ref,
    route_ref,
    out_ref,
    relay_ref,
    x_v,
    wqkv_v,
    kvp_v,
    wos_v,
    wot_v,
    wo_v,
    cache_v,
    zsend_v,
    zrecv_v,
    xsend_v,
    ysend_v,
    proj_v,
    q_v,
    nkv_v,
    att_v,
    acc_v,
    top_v,
    den_v,
    cos_v,
    sin_v,
    begin_v,
    out_v,
    local_sem,
    g_send,
    g_recv,
    t_send,
    t_recv,
    x_send,
    x_recv,
    z_send,
    z_recv,
    f_sem,
    o_sem,
    r_send,
    r_recv,
    n_send,
    n_recv,
    a_send,
    a_recv,
):
    tok_rows, depth = x_v.shape
    rows, q_cols = wq_hbm.shape
    own_rows = pl.ds(pl.multiple_of(lax.axis_index("wide") * rows, 64), rows)
    half_layers = xsend_v.shape[1]
    w = lax.axis_index("wide")
    n = lax.axis_index("narrow")
    core = lax.rem(w, 2)
    y = lax.rem(w // 2, 4)
    zh = w // 8
    plane = zh * 8

    def at_y(step):
        return plane + lax.rem(y + step, 4) * 2 + core

    def sib(chunk):
        return chunk + 1 - 2 * core

    def over_z(chunk):
        return lax.rem(chunk + 8, 16)

    yr, yl, y2 = at_y(1), at_y(3), at_y(2)
    zw, zr, zl, z2 = over_z(w), over_z(yr), over_z(yl), over_z(y2)
    sw = sib(w)
    par = lax.rem(n, 2)
    partner = n + 1 - 2 * par
    x_at, z_at = lax.rem(n, 4), n // 4

    def mix(one, other):
        return one + other - 2 * one * other

    shift_w = mix(zh, z_at) * 8 + lax.rem(y + x_at, 4) * 2 + core
    shifts = n > 0
    turn_n = mix(zh, z_at) * 4 + lax.rem(y - x_at + 4, 4)
    turns = turn_n != n

    half_at = pl.multiple_of(par * HEAD, HEAD)
    copies = [
        pltpu.make_async_copy(tok_hbm, x_v, local_sem.at[0]),
        pltpu.make_async_copy(wq_hbm, wqkv_v.at[own_rows, pl.ds(0, q_cols)], local_sem.at[1]),
        pltpu.make_async_copy(cache_hbm, cache_v, local_sem.at[2]),
        pltpu.make_async_copy(cache_hbm.at[0], kvp_v.at[w], local_sem.at[3]),
        pltpu.make_async_copy(
            wkv_hbm, wqkv_v.at[own_rows, pl.ds(q_cols, wkv_hbm.shape[1])], local_sem.at[7]
        ),
    ]
    for copy in copies:
        copy.start()

    barrier = pltpu.get_barrier_semaphore()

    def greet_wide(k, carry):
        pl.semaphore_signal(barrier, inc=1, device_id=(lax.rem(w + k, WIDE), n), device_id_type=MESH)
        return carry

    def greet_narrow(k, carry):
        pl.semaphore_signal(barrier, inc=1, device_id=(w, lax.rem(n + k, NARROW)), device_id_type=MESH)
        return carry

    lax.fori_loop(1, WIDE, greet_wide, 0)
    lax.fori_loop(1, NARROW, greet_narrow, 0)

    pl.semaphore_wait(barrier, WIDE - 1 + NARROW - 1)

    def shift_copy():
        return pltpu.make_async_remote_copy(
            src_ref=wo_hbm, dst_ref=wos_v, send_sem=t_send.at[0], recv_sem=t_recv.at[0],
            device_id=(shift_w, n), device_id_type=MESH,
        )

    def turn_copy():
        return pltpu.make_async_remote_copy(
            src_ref=wos_v, dst_ref=wot_v, send_sem=t_send.at[1], recv_sem=t_recv.at[1],
            device_id=(w, turn_n), device_id_type=MESH,
        )

    def shift_here():
        return pltpu.make_async_copy(wo_hbm, wos_v, local_sem.at[4])

    def turn_here():
        return pltpu.make_async_copy(wos_v, wot_v, local_sem.at[6])

    def either(moves, far, here):
        @pl.when(moves)
        def _():
            far()

        @pl.when(jnp.logical_not(moves))
        def _():
            here()

    either(shifts, lambda: shift_copy().start(), lambda: shift_here().start())

    def row_view(ref):
        def view(chunk, part=None):
            first = pl.multiple_of(chunk * rows, 64)
            if part is None:
                return ref.at[pl.ds(first, rows)]
            return ref.at[pl.ds(pl.multiple_of(first + part * (rows // 2), 32), rows // 2)]

        return view

    def prompt_view(chunk, part=None):
        return kvp_v.at[chunk] if part is None else kvp_v.at[chunk, part]

    views = [row_view(wqkv_v), prompt_view, row_view(wo_v)]
    owns = [None, cache_hbm.at[0], wot_v]
    started = []

    def message(a, kind, chunk, part, to, own=False):
        dst = views[a](chunk, part)
        return pltpu.make_async_remote_copy(
            src_ref=owns[a] if own and a > 0 else dst,
            dst_ref=dst,
            send_sem=g_send.at[a, kind],
            recv_sem=g_recv.at[a, kind],
            device_id=(to, n),
            device_id_type=MESH,
        )

    def send(a, kind, chunk, part, to, own=False):
        message(a, kind, chunk, part, to, own).start()
        started.append((a, kind, chunk, part, to, own))

    def arrived(a, kind, chunk, part=None):
        message(a, kind, chunk, part, w).wait_recv()

    def first(a):
        send(a, 1, w, None, zw, True)
        send(a, 2, w, None, yr, True)
        send(a, 3, w, None, yl, True)
        send(a, 0, w, None, sw, True)

    def second(a):
        arrived(a, 1, zw)
        send(a, 5, zw, None, yr)
        send(a, 6, zw, None, yl)
        send(a, 4, zw, None, sw)

    def third(a):
        arrived(a, 2, yl)
        send(a, 8, yl, 0, yr)
        send(a, 7, yl, None, sw)
        arrived(a, 3, yr)
        send(a, 10, yr, 1, yl)
        send(a, 9, yr, None, sw)

    def fourth(a):
        arrived(a, 5, zl)
        send(a, 12, zl, 0, yr)
        send(a, 11, zl, None, sw)
        arrived(a, 6, zr)
        send(a, 14, zr, 1, yl)
        send(a, 13, zr, None, sw)

    def fifth(a):
        arrived(a, 8, y2, 0)
        arrived(a, 10, y2, 1)
        send(a, 15, y2, None, sw)
        arrived(a, 12, z2, 0)
        arrived(a, 14, z2, 1)
        send(a, 16, z2, None, sw)

    def finish(a):
        for kind, chunk in (
            (0, w), (4, over_z(w)), (7, yl), (9, yr),
            (11, over_z(yl)), (13, over_z(yr)), (15, y2), (16, over_z(y2)),
        ):
            arrived(a, kind, sib(chunk))

    copies[1].wait()
    copies[4].wait()
    first(0)
    first(1)

    own_half = pl.ds(par * half_layers, half_layers)
    partner_half = pl.ds((1 - par) * half_layers, half_layers)
    own_lanes = pl.ds(half_at, HEAD)

    def z_copy(p):
        at = pl.ds(p * PAIR, PAIR)
        return pltpu.make_async_remote_copy(
            src_ref=zsend_v.at[at], dst_ref=zrecv_v.at[at],
            send_sem=z_send.at[p], recv_sem=z_recv.at[p],
            device_id=(over_z(w), n), device_id_type=MESH,
        )

    def near_x_copy():
        return pltpu.make_async_remote_copy(
            src_ref=xsend_v, dst_ref=ysend_v.at[0, :, :, :, :, own_lanes],
            send_sem=x_send.at[PAIRS], recv_sem=x_recv.at[PAIRS],
            device_id=(w, partner), device_id_type=MESH,
        )

    def far_x_copy(p):
        at = pl.ds(p * PAIR, PAIR)
        return pltpu.make_async_remote_copy(
            src_ref=zrecv_v.at[at, partner_half], dst_ref=ysend_v.at[1, at, :, :, :, own_lanes],
            send_sem=x_send.at[p], recv_sem=x_recv.at[p],
            device_id=(w, partner), device_id_type=MESH,
        )

    def far_own_copy(p):
        at = pl.ds(p * PAIR, PAIR)
        return pltpu.make_async_copy(
            zrecv_v.at[at, own_half], ysend_v.at[1, at, :, :, :, own_lanes], f_sem.at[p]
        )

    def page_for(to):
        page = jnp.int32(0)
        for t in range(WIDE):
            page = jnp.where(route_ref[0, t] == to, jnp.int32(t), page)
        return page

    copies[2].wait()

    def lay_far(d, carry):
        zsend_v[d] = cache_v[:, :, page_for(over_z(plane) + d)]
        return carry

    def lay_near(d, carry):
        page = page_for(plane + d)
        xsend_v[d] = cache_v[partner_half, :, page]
        ysend_v[0, d, :, :, :, own_lanes] = cache_v[own_half, :, page]
        return carry

    lax.fori_loop(0, PLANE, lay_far, 0)
    lax.fori_loop(0, PLANE, lay_near, 0)

    def to_partner(p, carry):
        z_copy(p).wait_recv()
        far_x_copy(p).start()
        far_own_copy(p).start()
        return carry

    tok_id = w * tok_rows + lax.broadcasted_iota(jnp.int32, (tok_rows, HEAD), 0)
    begin = jnp.zeros((tok_rows, HEAD), jnp.int32)
    off = jnp.zeros((tok_rows, HEAD), jnp.int32)
    edge = jnp.int32(0)
    for k in range(REQUESTS):
        inside = tok_id >= edge
        begin = jnp.where(inside, edge, begin)
        off = jnp.where(inside, starts_ref[k] - edge, off)
        edge = edge + lengths_ref[k]
    begin_v[...] = begin
    block_keys = kvp_v.shape[2] * kvp_v.shape[3]
    prompt_len = WIDE * block_keys
    angle = (prompt_len + off + tok_id).astype(F32) * freq_ref[...]
    cos_v[...] = jnp.cos(angle)
    lane = lax.broadcasted_iota(jnp.int32, (tok_rows, HEAD), 1)
    sin_v[...] = jnp.where(lane < HEAD // 2, -1.0, 1.0) * jnp.sin(angle)

    copies[0].wait()
    block = 32

    def norm_block(i, carry):
        at = pl.ds(pl.multiple_of(i * block, block), block)
        xf = x_v[at, :].astype(F32)
        mean = jnp.sum(xf * xf, -1, keepdims=True) * (1.0 / depth)
        x_v[at, :] = (xf * lax.rsqrt(mean + 1e-06) * gain_ref[...]).astype(BF16)
        return carry

    lax.fori_loop(0, tok_rows // block, norm_block, 0)

    either(shifts, lambda: shift_copy().wait_recv(), lambda: shift_here().wait())
    either(turns, lambda: turn_copy().start(), lambda: turn_here().start())
    second(0)
    third(0)
    z_copy(0).start()
    second(1)
    fourth(0)
    third(1)
    z_copy(1).start()
    either(turns, lambda: turn_copy().wait_recv(), lambda: turn_here().wait())
    first(2)
    own_wo2 = pltpu.make_async_copy(wot_v, views[2](w), local_sem.at[5])
    own_wo2.start()
    near_x_copy().start()
    fifth(0)
    finish(0)
    fourth(1)
    second(2)
    z_copy(2).start()
    z_copy(3).start()

    proj_v[...] = jnp.zeros_like(proj_v)
    step = 1280

    def project(i, carry):
        at = pl.ds(pl.multiple_of(i * step, step), step)
        proj_v[...] += jnp.dot(x_v[:, at], wqkv_v[at, :], preferred_element_type=F32)
        return carry

    lax.fori_loop(0, depth // step, project, 0)

    def rotated(heads, times=1.0):
        turned = heads * cos_v[...] + pltpu.roll(heads, HEAD // 2, 1) * sin_v[...]
        return (turned * times).astype(BF16)

    nkv_v[0, core, 0] = rotated(proj_v[:, GROUP * HEAD : (GROUP + 1) * HEAD])
    nkv_v[0, core, 1] = proj_v[:, (GROUP + 1) * HEAD : (GROUP + 2) * HEAD].astype(BF16)

    def back_copy(kind, slot, slot_to, which, to):
        return pltpu.make_async_remote_copy(
            src_ref=nkv_v.at[slot, which], dst_ref=nkv_v.at[slot_to, which],
            send_sem=n_send.at[kind], recv_sem=n_recv.at[kind],
            device_id=(to, n), device_id_type=MESH,
        )

    back_copies = [
        back_copy(1, 0, 1, core, lax.rem(w + 2, WIDE)),
        back_copy(2, 0, 2, core, lax.rem(w + 4, WIDE)),
        back_copy(0, 0, 0, core, sib(w)),
        back_copy(3, 1, 1, core, sib(w)),
        back_copy(4, 2, 2, core, sib(w)),
    ]
    for copy in back_copies[:3]:
        copy.start()
    factor = HEAD ** (-0.5) * LOG2E
    for h in range(GROUP):
        q_v[h] = rotated(proj_v[:, h * HEAD : (h + 1) * HEAD], factor)

    third(2)
    back_copies[0].wait_recv()
    back_copies[3].start()
    fifth(1)
    back_copies[1].wait_recv()
    back_copies[4].start()
    lax.fori_loop(0, PAIRS // 2, to_partner, 0)

    place = w - plane

    def source_of(s):
        return w if s == 0 else over_z(w)

    def y_copy(s, k, d, source):
        return pltpu.make_async_remote_copy(
            src_ref=ysend_v.at[s, d], dst_ref=relay_ref.at[0, :, :, source],
            send_sem=r_send.at[s, k], recv_sem=r_recv.at[s, k],
            device_id=(plane + d, n), device_id_type=MESH,
        )

    def to_owners(s):
        def step(k, carry):
            y_copy(s, k, lax.rem(place + k, PLANE), source_of(s)).start()
            return carry

        lax.fori_loop(1, PLANE, step, 0)

    def own_page(s):
        return pltpu.make_async_copy(
            ysend_v.at[s, place], relay_ref.at[0, :, :, source_of(s)], o_sem.at[s]
        )

    near_x_copy().wait_recv()
    to_owners(0)
    own_page(0).start()
    finish(1)
    copies[3].wait()
    for kind, slot, copy in ((0, 0, 2), (3, 1, 3), (4, 2, 4)):
        back_copy(kind, slot, slot, 1 - core, sib(w)).wait_recv()

    def scores(h, keys):
        return lax.dot_general(q_v[h], keys, (((1,), (1,)), ((), ())), preferred_element_type=F32)

    def attend(score, vals):
        top = top_v[...]
        new_top = jnp.maximum(top, jnp.max(score, 1, keepdims=True))
        fall = jnp.exp2(top - new_top)
        weight = jnp.exp2(score - new_top[:, :1]).astype(BF16)
        both = jnp.concatenate([vals, jnp.ones(vals.shape, BF16)], 1)
        summed = jnp.dot(weight, both, preferred_element_type=F32)
        acc_v[...] = acc_v[...] * fall + summed[:, :HEAD]
        den_v[...] = den_v[...] * fall + summed[:, HEAD:]
        top_v[...] = new_top

    per_step = KEYS // block_keys
    ring = (n // 4) * 4
    across = lax.rem(n + 4, NARROW)

    def around(k):
        return ring + lax.rem(n + k, 4)

    far_ring = 4 - ring

    def beyond(k):
        return far_ring + lax.rem(n + k, 4)

    lead, trail = around(1), around(3)

    def head_copy(h, kind, owner, to):
        lanes = pl.ds(pl.multiple_of(h * HEAD, HEAD), HEAD)
        if kind < 5:
            at = att_v.at[owner, :, lanes]
        else:
            at = att_v.at[owner, pl.ds((kind + 1) % 2 * (tok_rows // 2), tok_rows // 2), lanes]
        return pltpu.make_async_remote_copy(
            src_ref=at, dst_ref=at, send_sem=a_send.at[h, kind], recv_sem=a_recv.at[h, kind],
            device_id=(w, to), device_id_type=MESH,
        )

    sends = (
        (0, n, lead, trail), (1, n, trail, lead), (2, n, across, across),
        (3, across, lead, beyond(3)), (4, across, trail, beyond(1)),
        (5, trail, lead, around(2)), (6, lead, trail, around(2)),
        (7, beyond(3), lead, beyond(2)), (8, beyond(1), trail, beyond(2)),
    )

    def give(h, *kinds):
        for kind in kinds:
            _, owner, to, _ = sends[kind]
            head_copy(h, kind, owner, to).start()

    def take(h, *kinds):
        for kind in kinds:
            head_copy(h, kind, sends[kind][3], n).wait_recv()

    def pass_on(h):
        take(h, 2)
        give(h, 3, 4)
        take(h, 0)
        give(h, 5)
        take(h, 1)
        give(h, 6)

    def pass_further(h):
        take(h, 3)
        give(h, 7)
        take(h, 4)
        give(h, 8)

    def head_step(h, carry):
        top_v[...] = jnp.full_like(top_v, -1e30)
        den_v[...] = jnp.zeros_like(den_v)
        acc_v[...] = jnp.zeros_like(acc_v)

        steps = WIDE // per_step

        def keys_at(i):
            return kvp_v[i * per_step : (i + 1) * per_step, 0].reshape(KEYS, HEAD)

        def vals_at(i):
            return kvp_v[i * per_step : (i + 1) * per_step, 1].reshape(KEYS, HEAD)

        slots = []
        for j in range(BACK + 1):
            source = lax.rem(w - j + WIDE, WIDE)
            slots.append((lax.rem(w // 2 - source // 2 + PLANE, PLANE), lax.rem(source, 2)))
        new_keys = jnp.concatenate([nkv_v[away, which, 0] for away, which in slots], 0)
        new_vals = jnp.concatenate([nkv_v[away, which, 1] for away, which in slots], 0)
        ahead = scores(h, keys_at(0))
        for i in range(steps):
            score = ahead
            ahead = scores(h, keys_at(i + 1) if i + 1 < steps else new_keys)
            attend(score, vals_at(i))
        score = ahead
        own_id = w * tok_rows + lax.broadcasted_iota(jnp.int32, (tok_rows, tok_rows), 0)
        masked = []
        for j in range(BACK + 1):
            key_id = (w - j) * tok_rows + lax.broadcasted_iota(jnp.int32, (tok_rows, tok_rows), 1)
            visible = key_id >= begin_v[:, :1]
            if j == 0:
                visible = visible & (key_id <= own_id)
            masked.append(jnp.where(visible, score[:, j * tok_rows : (j + 1) * tok_rows], -1e30))
        attend(jnp.concatenate(masked, 1), new_vals)
        att_v[n, :, pl.ds(pl.multiple_of(h * HEAD, HEAD), HEAD)] = (acc_v[...] / den_v[...]).astype(BF16)
        give(h, 2, 0, 1)

        @pl.when(h > 0)
        def _():
            pass_on(h - 1)

        @pl.when(h > 1)
        def _():
            pass_further(h - 2)

        @pl.when(h == 0)
        def _():
            fourth(2)
            lax.fori_loop(PAIRS // 2, PAIRS, to_partner, 0)

        @pl.when(h == 2)
        def _():
            fifth(2)

            def far_ready(p, inner):
                far_x_copy(p).wait_recv()
                far_own_copy(p).wait()
                return inner

            lax.fori_loop(0, PAIRS, far_ready, 0)
            to_owners(1)
            own_page(1).start()

        return carry

    lax.fori_loop(0, GROUP, head_step, 0)
    last = GROUP - 1
    pass_further(last - 1)
    pass_on(last)

    finish(2)
    own_wo2.wait()
    out_v[...] = jnp.zeros_like(out_v)
    span = out_v.shape[1]

    early = last * HEAD

    def earlier(h, carry):
        take(h, 5, 6, 7, 8)
        return carry

    lax.fori_loop(0, last, earlier, 0)

    def out_step(owner, carry, at=0, size=early):
        held = mix(owner // 4, z_at) * 4 + lax.rem(owner + x_at, 4)
        rows_at = pl.ds(pl.multiple_of(held * span, span), span)
        out_v[...] += lax.dot_general(
            att_v[owner, :, at : at + size], wo_v[rows_at, at : at + size],
            (((1,), (1,)), ((), ())), preferred_element_type=F32,
        )
        return carry

    lax.fori_loop(0, NARROW // 2, out_step, 0)
    pass_further(last)
    lax.fori_loop(NARROW // 2, NARROW, out_step, 0)
    take(last, 5, 6, 7, 8)
    lax.fori_loop(0, NARROW, lambda owner, carry: out_step(owner, carry, early, HEAD), 0)
    out_ref[...] = out_v[...].astype(BF16)

    def sent(h, carry):
        for kind, owner, to, _ in sends:
            head_copy(h, kind, owner, to).wait_send()
        return carry

    lax.fori_loop(0, GROUP, sent, 0)
    for sending in started:
        message(*sending).wait_send()
    for copy in back_copies:
        copy.wait_send()

    either(shifts, lambda: shift_copy().wait_send(), lambda: None)
    either(turns, lambda: turn_copy().wait_send(), lambda: None)

    def far_sent(p, carry):
        z_copy(p).wait_send()
        far_x_copy(p).wait_send()
        return carry

    lax.fori_loop(0, PAIRS, far_sent, 0)
    near_x_copy().wait_send()
    for s in range(2):
        own_page(s).wait()

        def relay_end(k, carry):
            y_copy(s, k, lax.rem(place + k, PLANE), source_of(s)).wait_send()
            giver = plane + lax.rem(place - k + PLANE, PLANE)
            y_copy(s, k, place, giver if s == 0 else over_z(giver)).wait_recv()
            return carry

        lax.fori_loop(1, PLANE, relay_end, 0)


def on_device(
    tokens,
    norm_gain,
    w_query,
    w_keyval,
    w_output,
    prompt_cache,
    stretch_lengths,
    stretch_starts,
    page_route,
):
    tok_rows, depth = tokens.shape
    rows, q_cols = w_query.shape
    layers, kinds, cache_rows, channels = prompt_cache.shape
    pages = page_route.shape[1]
    page_rows = cache_rows // pages
    half = layers // 2
    cols = q_cols + 2 * channels
    freq = 1000000.0 ** (-np.arange(HEAD // 2) * 2.0 / HEAD)
    freq = jnp.asarray(np.concatenate([freq, freq])[None], jnp.float32)
    any_spec = pl.BlockSpec(memory_space=pl.ANY)
    vmem_spec = pl.BlockSpec(memory_space=pltpu.VMEM)
    smem_spec = pl.BlockSpec(memory_space=pltpu.SMEM)
    cache5 = prompt_cache.reshape(layers, kinds, pages, page_rows, channels)
    dma = pltpu.SemaphoreType.DMA
    attn_out, relay = pl.pallas_call(
        whole_kernel,
        out_shape=(
            jax.ShapeDtypeStruct((tok_rows, q_cols), BF16),
            jax.ShapeDtypeStruct((1, half, kinds, WIDE, page_rows, 2 * channels), BF16),
        ),
        in_specs=[
            any_spec, vmem_spec, any_spec, any_spec, any_spec, any_spec, vmem_spec,
            smem_spec, smem_spec, smem_spec,
        ],
        out_specs=(vmem_spec, any_spec),
        scratch_shapes=[
            pltpu.VMEM((tok_rows, depth), BF16),
            pltpu.VMEM((WIDE * rows, cols), BF16),
            pltpu.VMEM((WIDE, kinds, pages, page_rows, channels), BF16),
            pltpu.VMEM((rows, q_cols), BF16),
            pltpu.VMEM((rows, q_cols), BF16),
            pltpu.VMEM((WIDE * rows, q_cols), BF16),
            pltpu.VMEM((layers, kinds, pages, page_rows, channels), BF16),
            pltpu.VMEM((PLANE, layers, kinds, page_rows, channels), BF16),
            pltpu.VMEM((PLANE, layers, kinds, page_rows, channels), BF16),
            pltpu.VMEM((PLANE, half, kinds, page_rows, channels), BF16),
            pltpu.VMEM((2, PLANE, half, kinds, page_rows, 2 * channels), BF16),
            pltpu.VMEM((tok_rows, cols), F32),
            pltpu.VMEM((GROUP, tok_rows, HEAD), BF16),
            pltpu.VMEM((3, 2, 2, tok_rows, HEAD), BF16),
            pltpu.VMEM((NARROW, tok_rows, q_cols), BF16),
            pltpu.VMEM((tok_rows, HEAD), F32),
            pltpu.VMEM((tok_rows, HEAD), F32),
            pltpu.VMEM((tok_rows, HEAD), F32),
            pltpu.VMEM((tok_rows, HEAD), F32),
            pltpu.VMEM((tok_rows, HEAD), F32),
            pltpu.VMEM((tok_rows, HEAD), jnp.int32),
            pltpu.VMEM((tok_rows, q_cols), F32),
            dma((8,)),
            dma((3, MESSAGES)),
            dma((3, MESSAGES)),
            dma((2,)),
            dma((2,)),
            dma((PAIRS + 1,)),
            dma((PAIRS + 1,)),
            dma((PAIRS,)),
            dma((PAIRS,)),
            dma((PAIRS,)),
            dma((2,)),
            dma((2, PLANE)),
            dma((2, PLANE)),
            dma((5,)),
            dma((5,)),
            dma((GROUP, 9)),
            dma((GROUP, 9)),
        ],
        compiler_params=pltpu.CompilerParams(
            collective_id=0, has_side_effects=True, vmem_limit_bytes=60 * 2**20
        ),
    )(
        tokens, norm_gain[None], w_query, w_keyval.reshape(rows, 2 * channels), w_output.T, cache5, freq,
        stretch_lengths, stretch_starts, page_route,
    )
    return attn_out, relay


def solution(mesh):
    placed = (
        P("wide", None),
        P(),
        P("wide", "narrow"),
        P("wide", None, "narrow"),
        P("narrow", "wide"),
        P(None, None, "wide", "narrow"),
        P(),
        P(),
        P("wide", None),
    )
    return jax.shard_map(
        on_device,
        mesh=mesh,
        in_specs=placed,
        out_specs=(P("wide", "narrow"), P("narrow", None, None, "wide", None, None)),
        check_vma=False,
    )
```
